256 devices in a mesh: dp: 32 (over y_lo, z, core), inner: 8 (over x, y_hi).
Axes of the slice: x: 4, y: 4 (y_hi: 2, y_lo: 2; y = y_hi * 2 + y_lo), z: 8, core: 2. Of those that a mesh axis runs over, the one named last changes fastest.
Arguments:
- queries: bfloat16 [65536, 4096], P(('dp', 'inner')), may hold values from -8 to 8
- documents: bfloat16 [65536, 4096], P(('dp', 'inner')), may hold values from -4 to 4
- positives: int32 [65536], P(('dp', 'inner')), may hold values from 0 to 65535, as said below
Outputs:
- row_terms: float32 [65536], P(('dp', 'inner'))
- query_grad: float32 [65536, 4096], P(('dp', 'inner'))
- doc_grad: float32 [65536, 4096], P(('dp', 'inner'))
The draws below stay inside these ranges and needn't reach their ends.
Inputs may be any that keep to these rules, and one draw needn't show every extreme that they name: positives maps each aligned block of 256 rows onto the same block, each row of it once.
All inputs are finite; a program needn't handle non-finite values.
Results may differ from the reference program's by a relative error of at most 0.0011.
Values may be sent and summed in bfloat16 or wider, within the bound.
No kernel may reach another device: no remote copies, remote signals or barrier semaphores. Data moves between devices by JAX's collectives and lax.ppermute only.
A program may use at most 128 MiB of HBM per device.

```python
import math
import jax
import jax.numpy as jnp
from jax import lax

D = 4096
ROW_DEV = 256
STEPS = 3
BATCH = 65536


def base_documents(key):
    return jnp.clip(jax.random.normal(key, (BATCH, D), jnp.float32), -4.0, 4.0)


def draw_documents(key, part):
    shared = base_documents(key)
    result = shared
    return result.astype(jnp.bfloat16)


def draw_queries(key, part):
    own_key = jax.random.fold_in(key, 5)
    result = jnp.clip(jax.random.normal(own_key, (BATCH, D), jnp.float32), -4.0, 4.0)
    return result.astype(jnp.bfloat16)


def draw_positives(key, part):
    key = jax.random.fold_in(key, 7)
    count = BATCH // ROW_DEV
    keys = jax.random.split(key, count)
    orders = jax.vmap(lambda single: jax.random.permutation(single, ROW_DEV))(keys)
    starts = (jnp.arange(count, dtype=jnp.int32) * ROW_DEV)[:, None]
    return (orders.astype(jnp.int32) + starts).reshape(BATCH).astype(jnp.int32)


def setup_inputs(seed: int = 0) -> dict:
    key_list = jax.random.split(jax.random.key(seed), 4)
    queries = draw_queries(jax.random.fold_in(key_list[3], 71), 0)
    documents = draw_documents(jax.random.fold_in(key_list[3], 71), 0)
    positives = draw_positives(jax.random.fold_in(key_list[3], 71), 0)
    return {"queries": queries, "documents": documents, "positives": positives}


NEGATIVE = -1e+30

def rounded(values):
    return lax.optimization_barrier(values.astype(jnp.bfloat16)).astype(jnp.float32)

def grams(left_rows, right_rows):
    return jnp.einsum('bik,bjk->bij', left_rows, right_rows, precision=lax.Precision.HIGHEST)

def apply_tile(coef, embed):
    return jnp.einsum('bij,bjk->bik', coef, embed, precision=lax.Precision.HIGHEST)

def apply_transposed(coef, embed):
    return jnp.einsum('bij,bik->bjk', coef, embed, precision=lax.Precision.HIGHEST)

def reference(queries, documents, positives):
    blocks = BATCH // ROW_DEV
    logit_scale = 2.0 / math.sqrt(D)
    query_blk = queries.astype(jnp.float32).reshape(blocks, ROW_DEV, D)
    doc_blk = documents.astype(jnp.float32).reshape(blocks, ROW_DEV, D)
    same_row = jnp.eye(ROW_DEV, dtype=bool)[None]
    local_pos = positives.reshape(blocks, ROW_DEV) - (jnp.arange(blocks, dtype=jnp.int32) * ROW_DEV)[:, None]
    is_positive = local_pos[:, :, None] == jnp.arange(ROW_DEV, dtype=jnp.int32)[None, None, :]
    cross_tiles, query_tiles, doc_tiles = ([], [], [])
    for offset in range(STEPS):
        far_q = jnp.roll(query_blk, -offset, axis=0)
        far_d = jnp.roll(doc_blk, -offset, axis=0)
        cross = logit_scale * grams(query_blk, far_d)
        query_pair = logit_scale * grams(query_blk, far_q)
        doc_pair = logit_scale * grams(doc_blk, far_d)
        if offset == 0:
            query_pair = jnp.where(same_row, NEGATIVE, query_pair)
            doc_pair = jnp.where(same_row, NEGATIVE, doc_pair)
        cross_tiles.append(cross)
        query_tiles.append(query_pair)
        doc_tiles.append(doc_pair)
    query_parts = cross_tiles + query_tiles + [jnp.swapaxes(jnp.roll(query_tiles[offset], offset, axis=0), 1, 2) for offset in range(1, STEPS)]
    doc_parts = [jnp.swapaxes(jnp.roll(cross_tiles[offset], offset, axis=0), 1, 2) for offset in range(STEPS)] + doc_tiles + [jnp.swapaxes(jnp.roll(doc_tiles[offset], offset, axis=0), 1, 2) for offset in range(1, STEPS)]
    query_lse = jax.nn.logsumexp(jnp.concatenate(query_parts, axis=2), axis=2)
    doc_lse = jax.nn.logsumexp(jnp.concatenate(doc_parts, axis=2), axis=2)
    positive = lax.optimization_barrier(jnp.sum(jnp.where(is_positive, cross_tiles[0], 0.0), axis=2))
    row_terms = (query_lse + doc_lse - 2.0 * positive).reshape(BATCH)
    grad_q = jnp.zeros_like(query_blk)
    grad_d = jnp.zeros_like(doc_blk)
    for offset in range(STEPS):
        far_q = jnp.roll(query_blk, -offset, axis=0)
        far_d = jnp.roll(doc_blk, -offset, axis=0)
        far_qlse = jnp.roll(query_lse, -offset, axis=0)
        far_dlse = jnp.roll(doc_lse, -offset, axis=0)
        cross = cross_tiles[offset]
        weight = jnp.exp(cross - query_lse[:, :, None]) + jnp.exp(cross - far_dlse[:, None, :])
        halving = 1.0
        if offset == 0:
            weight = weight - 2.0 * is_positive.astype(jnp.float32)
            halving = 0.5
        coef_qq = halving * (jnp.exp(query_tiles[offset] - query_lse[:, :, None]) + jnp.exp(query_tiles[offset] - far_qlse[:, None, :]))
        coef_dd = halving * (jnp.exp(doc_tiles[offset] - doc_lse[:, :, None]) + jnp.exp(doc_tiles[offset] - far_dlse[:, None, :]))
        weight = rounded(weight)
        coef_qq = rounded(coef_qq)
        coef_dd = rounded(coef_dd)
        grad_q = grad_q + apply_tile(weight, far_d) + apply_tile(coef_qq, far_q)
        grad_d = grad_d + apply_tile(coef_dd, far_d)
        back_q = apply_transposed(coef_qq, query_blk)
        back_d = apply_transposed(weight, query_blk) + apply_transposed(coef_dd, doc_blk)
        grad_q = grad_q + jnp.roll(back_q, offset, axis=0)
        grad_d = grad_d + jnp.roll(back_d, offset, axis=0)
    factor = logit_scale / (2.0 * BATCH)
    return (row_terms, (factor * grad_q).reshape(BATCH, D), (factor * grad_d).reshape(BATCH, D))
```

```python
import math

import jax
import jax.numpy as jnp
from jax import lax
from jax.experimental import pallas as pl
from jax.experimental.pallas import tpu as pltpu
from jax.sharding import PartitionSpec as P

AXES = ("dp", "inner")
NEGATIVE = -1e30
CHUNK = 512
VMEM_LIMIT = 50 * 1024 * 1024


def contract(left_rows, right_rows):
    return lax.dot_general(
        left_rows, right_rows, (((1,), (1,)), ((), ())), preferred_element_type=jnp.float32
    )


def sent(value, target, senders=None):
    count = lax.axis_size(AXES)
    senders = range(count) if senders is None else senders
    return lax.ppermute(value, AXES, [(i, target(i) % count) for i in senders])


def down_hop(half):
    return lambda i: i - half if i >= half else (i ^ 1) + half


def up_hop(half):
    return lambda i: (i - half) ^ 1 if i >= half else i + half


def within_half(half, step):
    return lambda i: i - i % half + (i + step) % half


def as_columns(row):
    size = row.shape[1]
    return jnp.broadcast_to(row, (size, size)).T


def statistics(tiles):
    largest = tiles[0]
    for tile in tiles[1:]:
        largest = jnp.maximum(largest, tile)
    largest = jnp.max(largest, axis=1, keepdims=True)
    total = jnp.exp(tiles[0] - largest)
    for tile in tiles[1:]:
        total = total + jnp.exp(tile - largest)
    lse = largest + jnp.log(jnp.sum(total, axis=1, keepdims=True))
    return jnp.broadcast_to(lse, tiles[0].shape).T[:1]


TILES = 24


def read_tiles(place, *refs):
    even, first, last, edge = [place[k] == 1 for k in range(4)]
    qq, qd, dq, dd, qq_n2, qd_n2, dd_n2, dq_p2, dd_p2, qq_p2 = [ref[...] for ref in refs[:10]]
    qq_pair, dq_pair, qd_pair, dd_pair, qq_edge, dq_edge = [ref[...] for ref in refs[10:16]]
    qd_low, dd_low, qd_high, dd_high, qq_diag, dq_diag, qq_swap, dq_swap = [
        ref[...] for ref in refs[16:]
    ]
    qd_diag = jnp.concatenate([qd_low, qd_high], axis=1)
    dd_diag = jnp.concatenate([dd_low, dd_high], axis=1)
    qq_diag = jnp.where(edge, qq_edge, qq_diag)
    dq_diag = jnp.where(edge, dq_edge, dq_diag)
    q_tiles = [
        jnp.where(last, qq_swap, qq_n2),
        jnp.where(even, qq_pair, qq_diag),
        qd,
        qq,
        qd_n2,
        jnp.where(first, qq_swap, qq_p2),
        jnp.where(even, qd_pair, qd_diag),
        jnp.where(even, qq_diag, qq_pair),
    ]
    d_tiles = [
        dd,
        dq,
        dd_n2,
        jnp.where(first, dq_swap, dq_p2),
        jnp.where(even, dd_pair, dd_diag),
        jnp.where(even, dq_diag, dq_pair),
        dd_p2,
        jnp.where(even, dd_diag, dd_pair),
    ]
    return q_tiles, d_tiles


def lse_kernel(place, pos, *refs):
    lse, row_terms = refs[TILES:]
    q_tiles, d_tiles = read_tiles(place, *refs[:TILES])
    q_row = statistics(q_tiles)
    d_row = statistics(d_tiles)
    lse[0:1, :] = q_row
    lse[1:2, :] = d_row
    cross = d_tiles[1]
    doc = lax.broadcasted_iota(jnp.int32, cross.shape, 0)
    positive = jnp.sum(jnp.where(doc == pos[...], cross, 0.0), axis=0, keepdims=True)
    row_terms[...] = q_row + d_row - 2.0 * positive


def grad_kernel(factor, place, pos, *refs):
    tiles, refs = refs[:TILES], refs[TILES:]
    lse, lse_n1, lse_p1, lse_n2, lse_p2 = refs[:5]
    own_q, own_d, q_n2, d_n2, q_p2, d_p2, q_pair, d_pair = refs[5:13]
    q_edge, d_low, d_high, q_diag, q_swap = refs[13:18]
    grad_q, grad_d, coef_q, coef_d, rows, arrived = refs[18:]
    step = pl.program_id(0)
    size = grad_q.shape[0]
    width = own_q.shape[1]
    chunk = rows.shape[2]
    even, first, last, edge = [place[k] == 1 for k in range(4)]

    def bring(source, slot, offset=0, taken=None):
        def start():
            for part in range(width // chunk):
                pltpu.make_async_copy(
                    source.at[:, pl.ds(part * chunk, chunk)],
                    rows.at[part, pl.ds(slot * size + offset, source.shape[0]), :],
                    arrived.at[part],
                ).start()

        if taken is None:
            start()
        else:
            pl.when(taken)(start)

    @pl.when(step == 0)
    def _():
        half = size // 2
        odd = jnp.logical_not(even)
        bring(own_d, 2)
        bring(own_q, 3)
        bring(d_n2, 4)
        bring(d_p2, 8)
        bring(q_n2, 0, taken=jnp.logical_not(last))
        bring(q_swap, 0, taken=last)
        bring(q_p2, 5, taken=jnp.logical_not(first))
        bring(q_swap, 5, taken=first)
        for turn, pair_slots, diag_slots in ((even, (1, 6), (7, 9)), (odd, (7, 9), (1, 6))):
            bring(q_pair, pair_slots[0], taken=turn)
            bring(d_pair, pair_slots[1], taken=turn)
            bring(q_diag, diag_slots[0], taken=turn & jnp.logical_not(edge))
            bring(q_edge, diag_slots[0], taken=turn & edge)
            bring(d_low, diag_slots[1], taken=turn)
            bring(d_high, diag_slots[1], half, taken=turn)

        q_tiles, d_tiles = read_tiles(place, *tiles)
        q_col = as_columns(lse[0:1, :])
        d_col = as_columns(lse[1:2, :])
        lane = lax.broadcasted_iota(jnp.int32, (size, size), 1)
        sublane = lax.broadcasted_iota(jnp.int32, (size, size), 0)
        pos_col = as_columns(pos[...])

        def put(target, slot, tile, column, row, taken=None):
            value = jnp.exp(tile - column) + jnp.exp(tile - row)
            if taken is not None:
                value = value - jnp.where(taken, 2.0, 0.0)
            target[:, slot * size : (slot + 1) * size] = value.astype(jnp.bfloat16)

        q_of = [ref[0:1, :] for ref in (lse_n2, lse_n1, lse, lse, lse_n2, lse_p2, lse_n1, lse_p1)]
        d_of = [ref[1:2, :] for ref in (lse_n2, lse_n1, lse, lse, lse_n2, lse_p2, lse_n1, lse_p1)]
        q_kind = [q_of, q_of, d_of, q_of, d_of, q_of, d_of, q_of]
        for slot in range(8):
            taken = pos_col == lane if slot == 2 else None
            put(coef_q, slot, q_tiles[slot], q_col, q_kind[slot][slot], taken)
        d_rows = [
            lse[1:2, :],
            lse[0:1, :],
            lse_n2[1:2, :],
            lse_p2[0:1, :],
            lse_n1[1:2, :],
            lse_p1[0:1, :],
            lse_p2[1:2, :],
            lse_p1[1:2, :],
        ]
        for slot in range(8):
            taken = pos[...] == sublane if slot == 1 else None
            put(coef_d, slot, d_tiles[slot], d_col, d_rows[slot], taken)

    pltpu.make_async_copy(rows.at[step], rows.at[step], arrived.at[step]).wait()
    depth = coef_q.shape[1]
    grad_q[...] = factor * jnp.dot(
        coef_q[...], rows[step, 0:depth, :], preferred_element_type=jnp.float32
    )
    grad_d[...] = factor * jnp.dot(
        coef_d[...], rows[step, 2 * size :, :], preferred_element_type=jnp.float32
    )


def per_device(queries, documents, positives):
    size, width = queries.shape
    count = lax.axis_size(AXES)
    scale = 2.0 / math.sqrt(width)
    factor = scale / (2.0 * size * count)
    own_block = lax.axis_index("dp") * lax.axis_size("inner") + lax.axis_index("inner")
    half = count // 2
    within = own_block % half
    first, last = within < 2, within >= half - 2
    place = jnp.stack(
        [own_block % 2 == 0, first, last, (within == 0) | (within == half - 1)]
    ).astype(jnp.int32)
    pos = (positives - own_block * size).reshape(1, size)
    index = jnp.arange(size)
    same_row = index[:, None] == index[None, :]
    down, up = down_hop(half), up_hop(half)

    q_down = sent(queries, down)
    d_up = sent(documents, up)
    d_p2 = sent(documents, lambda i: i + 2)
    d_n2 = sent(documents, lambda i: i - 2)
    q_edge = sent(
        queries,
        lambda i: i - 1 if i % half == 0 else i + 1,
        [0, half - 1, half, count - 1],
    )
    q_down, d_up = lax.optimization_barrier((q_down, d_up))
    q_pair = sent(q_down, down)
    d_pair = sent(d_up, up)
    q_own, d_p2, d_n2, q_edge, q_down, d_up = lax.optimization_barrier(
        (queries, d_p2, d_n2, q_edge, q_down, d_up)
    )
    q_p2 = sent(q_own, within_half(half, 2))
    q_n2 = sent(q_own, within_half(half, -2))
    d_turn = jnp.where(own_block % 2 == 0, d_n2, d_p2)
    q_diag = sent(q_pair, lambda i: within_half(half, -2 if i % 2 else 2)(i))
    d_turn, d_pair = lax.optimization_barrier((d_turn, d_pair))
    d_low = sent(d_turn[: size // 2], up)
    d_high = sent(d_turn[size // 2 :], down)
    d_low, d_high, q_n2, q_p2 = lax.optimization_barrier((d_low, d_high, q_n2, q_p2))
    d_low = sent(d_low, up)
    d_high = sent(d_high, down)
    q_swap = sent(
        jnp.where(last, q_n2, q_p2),
        lambda i: i + half,
        [i for i in range(count) if i % half < 2 or i % half >= half - 2],
    )

    def tile(left, right):
        return scale * contract(left, right)

    def masked(tile):
        return jnp.where(same_row, NEGATIVE, tile)

    tiles = [
        masked(tile(queries, queries)),
        tile(queries, documents),
        tile(documents, queries),
        masked(tile(documents, documents)),
        tile(queries, q_n2),
        tile(queries, d_n2),
        tile(documents, d_n2),
        tile(documents, q_p2),
        tile(documents, d_p2),
        tile(queries, q_p2),
        tile(queries, q_pair),
        tile(documents, q_pair),
        tile(queries, d_pair),
        tile(documents, d_pair),
        tile(queries, q_edge),
        tile(documents, q_edge),
        tile(queries, d_low),
        tile(documents, d_low),
        tile(queries, d_high),
        tile(documents, d_high),
        tile(queries, q_diag),
        tile(documents, q_diag),
        tile(queries, q_swap),
        tile(documents, q_swap),
    ]
    in_vmem = pl.BlockSpec(memory_space=pltpu.VMEM)
    in_smem = pl.BlockSpec(memory_space=pltpu.SMEM)
    anywhere = pl.BlockSpec(memory_space=pl.ANY)
    lse, row_terms = pl.pallas_call(
        lse_kernel,
        out_shape=(
            jax.ShapeDtypeStruct((2, size), jnp.float32),
            jax.ShapeDtypeStruct((1, size), jnp.float32),
        ),
        in_specs=[in_smem] + [in_vmem] * (1 + TILES),
        out_specs=(in_vmem, in_vmem),
        compiler_params=pltpu.CompilerParams(vmem_limit_bytes=VMEM_LIMIT),
        cost_estimate=pl.CostEstimate(
            flops=0, bytes_accessed=18 * size * size * 4, transcendentals=16 * size * size
        ),
    )(place, pos, *tiles)
    lse_n1 = sent(lse, lambda i: i - 1)
    lse_p1 = sent(lse, lambda i: i + 1)
    lse_n2 = sent(lse, lambda i: i - 2)
    lse_p2 = sent(lse, lambda i: i + 2)
    sources = [queries, documents, q_n2, d_n2, q_p2, d_p2, q_pair, d_pair]
    sources += [q_edge, d_low, d_high, q_diag, q_swap]
    parts = width // CHUNK

    def kernel(*refs):
        grad_kernel(factor, *refs)

    grad_block = pl.BlockSpec((size, CHUNK), lambda step: (0, step))
    grad_q, grad_d = pl.pallas_call(
        kernel,
        grid=(parts,),
        out_shape=(jax.ShapeDtypeStruct((size, width), jnp.float32),) * 2,
        in_specs=[in_smem] + [in_vmem] * (6 + TILES) + [anywhere] * len(sources),
        out_specs=(grad_block, grad_block),
        scratch_shapes=[
            pltpu.VMEM((size, 8 * size), jnp.bfloat16),
            pltpu.VMEM((size, 8 * size), jnp.bfloat16),
            pltpu.VMEM((parts, 10 * size, CHUNK), jnp.bfloat16),
            pltpu.SemaphoreType.DMA((parts,)),
        ],
        compiler_params=pltpu.CompilerParams(vmem_limit_bytes=VMEM_LIMIT),
        cost_estimate=pl.CostEstimate(
            flops=2 * 16 * size * size * width,
            bytes_accessed=(20 + 8) * size * width,
            transcendentals=32 * size * size,
        ),
    )(place, pos, *tiles, lse, lse_n1, lse_p1, lse_n2, lse_p2, *sources)
    return (row_terms.reshape(size), grad_q, grad_d)


def solution(mesh):
    placed = (P(AXES, None), P(AXES, None), P(AXES))
    return jax.shard_map(
        per_device,
        mesh=mesh,
        in_specs=placed,
        out_specs=(P(AXES), P(AXES, None), P(AXES, None)),
        check_vma=False,
    )
```

```python
import math

import jax
import jax.numpy as jnp
from jax import lax
from jax.experimental import pallas as pl
from jax.experimental.pallas import tpu as pltpu
from jax.sharding import PartitionSpec as P

AXES = ("dp", "inner")
NEGATIVE = -1e30
CHUNK = 1024
VMEM_LIMIT = 46 * 1024 * 1024
SMALL_LIMIT = 16 * 1024 * 1024


def contract(left_rows, right_rows):
    return lax.dot_general(
        left_rows, right_rows, (((1,), (1,)), ((), ())), preferred_element_type=jnp.float32
    )


def sent(value, target, senders=None):
    count = lax.axis_size(AXES)
    senders = range(count) if senders is None else senders
    return lax.ppermute(value, AXES, [(i, target(i) % count) for i in senders])


def down_hop(half):
    return lambda i: i - half if i >= half else (i ^ 1) + half


def up_hop(half):
    return lambda i: (i - half) ^ 1 if i >= half else i + half


def as_columns(row):
    size = row.shape[1]
    return jnp.broadcast_to(row, (size, size)).T


def peak_and_sum(tiles):
    largest = tiles[0]
    for tile in tiles[1:]:
        largest = jnp.maximum(largest, tile)
    largest = jnp.max(largest, axis=1, keepdims=True)
    total = jnp.exp(tiles[0] - largest)
    for tile in tiles[1:]:
        total = total + jnp.exp(tile - largest)
    return largest, jnp.sum(total, axis=1, keepdims=True)


def early_kernel(scale, place, pos, *refs):
    qq, qd, dq, dd, qd_n2, dd_n2, dd_p2 = refs[:7]
    own_q, own_d, q_n2, q_p2, q_pair, d_pair = refs[7:13]
    qq_n2, dq_p2, qq_p2, qq_pair, cross_pair, dd_pair = refs[13:19]
    q_max, q_sum, d_max, d_sum, positive = refs[19:]
    even, first, last = [place[k] == 1 for k in range(3)]
    qq_pair[...] = scale * contract(own_q[...], q_pair[...])
    dd_pair[...] = scale * contract(own_d[...], d_pair[...])
    qq_n2[...] = scale * contract(own_q[...], q_n2[...])
    qq_p2[...] = scale * contract(own_q[...], q_p2[...])
    dq_p2[...] = scale * contract(own_d[...], q_p2[...])

    @pl.when(even)
    def _():
        cross_pair[...] = scale * contract(own_q[...], d_pair[...])

    @pl.when(jnp.logical_not(even))
    def _():
        cross_pair[...] = scale * contract(own_d[...], q_pair[...])

    cross = cross_pair[...]
    q_tiles = [
        qd[...],
        qq[...],
        qd_n2[...],
        qq_pair[...],
        jnp.where(last, NEGATIVE, qq_n2[...]),
        jnp.where(first, NEGATIVE, qq_p2[...]),
        jnp.where(even, cross, NEGATIVE),
    ]
    d_tiles = [
        dd[...],
        dq[...],
        dd_n2[...],
        dd_p2[...],
        dd_pair[...],
        jnp.where(first, NEGATIVE, dq_p2[...]),
        jnp.where(even, NEGATIVE, cross),
    ]
    for tiles, out_max, out_sum in ((q_tiles, q_max, q_sum), (d_tiles, d_max, d_sum)):
        largest, total = peak_and_sum(tiles)
        out_max[...] = jnp.broadcast_to(largest, out_max.shape)
        out_sum[...] = jnp.broadcast_to(total, out_sum.shape)
    doc = lax.broadcasted_iota(jnp.int32, dq.shape, 0)
    positive[...] = jnp.sum(jnp.where(doc == pos[...], dq[...], 0.0), axis=0, keepdims=True)


def lse_kernel(scale, place, qq_edge, dq_edge, q_max, q_sum, d_max, d_sum, positive, *refs):
    own_q, own_d, q_diag, d_low, d_high, q_swap = refs[:6]
    qq_diag, cross_diag, dd_diag, qq_swap, dq_swap, lse, row_terms = refs[6:]
    even, first, last, edge = [place[k] == 1 for k in range(4)]
    half = d_low.shape[1]

    def with_documents(own):
        return scale * (contract(own[:, :half], d_low[...]) + contract(own[:, half:], d_high[...]))

    qq_diag[...] = jnp.where(edge, qq_edge[...], scale * contract(own_q[...], q_diag[...]))
    dd_diag[...] = with_documents(own_d)

    @pl.when(even)
    def _():
        cross_diag[...] = jnp.where(edge, dq_edge[...], scale * contract(own_d[...], q_diag[...]))

    @pl.when(jnp.logical_not(even))
    def _():
        cross_diag[...] = with_documents(own_q)

    @pl.when(first | last)
    def _():
        qq_swap[...] = scale * contract(own_q[...], q_swap[...])
        dq_swap[...] = scale * contract(own_d[...], q_swap[...])

    @pl.when(jnp.logical_not(first | last))
    def _():
        qq_swap[...] = jnp.full(qq_swap.shape, NEGATIVE, jnp.float32)
        dq_swap[...] = jnp.full(dq_swap.shape, NEGATIVE, jnp.float32)

    def finished(early_max, early_sum, tiles):
        largest = early_max[:, :1]
        for tile in tiles:
            largest = jnp.maximum(largest, jnp.max(tile, axis=1, keepdims=True))
        total = jnp.exp(tiles[0] - largest)
        for tile in tiles[1:]:
            total = total + jnp.exp(tile - largest)
        total = jnp.sum(total, axis=1, keepdims=True)
        total = total + early_sum[:, :1] * jnp.exp(early_max[:, :1] - largest)
        return jnp.broadcast_to(largest + jnp.log(total), tiles[0].shape).T[:1]

    cross = cross_diag[...]
    q_late = [qq_diag[...], qq_swap[...], jnp.where(even, NEGATIVE, cross)]
    d_late = [dd_diag[...], jnp.where(first, dq_swap[...], NEGATIVE), jnp.where(even, cross, NEGATIVE)]
    q_row = finished(q_max, q_sum, q_late)
    d_row = finished(d_max, d_sum, d_late)
    lse[0:1, :] = q_row
    lse[1:2, :] = d_row
    row_terms[...] = q_row + d_row - 2.0 * positive[...]


TILES = 18


def grad_kernel(factor, place, pos, *refs):
    tiles, refs = refs[:TILES], refs[TILES:]
    lse, lse_n1, lse_p1, lse_n2, lse_p2 = refs[:5]
    own_q, own_d, q_n2, d_n2, q_p2, d_p2, q_pair, d_pair = refs[5:13]
    q_edge, d_low, d_high, q_diag, q_swap = refs[13:18]
    grad_q, grad_d, coef_q, coef_d, rows, arrived = refs[18:]
    step = pl.program_id(0)
    size = grad_q.shape[0]
    width = own_q.shape[1]
    chunk = rows.shape[2]
    parts = width // chunk
    even, first, last, edge = [place[k] == 1 for k in range(4)]

    def bring(part):
        def one(source, slot, column=part * chunk):
            start = slot * size if isinstance(slot, int) else pl.multiple_of(slot * size, size)
            pltpu.make_async_copy(
                source.at[:, pl.ds(column, chunk)],
                rows.at[part, pl.ds(start, size), :],
                arrived.at[part],
            ).start()

        def either(taken, yes, no, slot):
            pl.when(taken)(lambda: one(yes, slot))
            pl.when(jnp.logical_not(taken))(lambda: one(no, slot))

        one(own_d, 2)
        one(own_q, 3)
        one(d_n2, 4)
        one(d_p2, 8)
        one(q_pair, jnp.where(even, 1, 7))
        one(d_pair, jnp.where(even, 6, 9))
        source = d_low if part < parts // 2 else d_high
        one(source, jnp.where(even, 9, 6), part % (parts // 2) * chunk)
        either(edge, q_edge, q_diag, jnp.where(even, 7, 1))
        either(last, q_swap, q_n2, 0)
        either(first, q_swap, q_p2, 5)

    @pl.when(step == 0)
    def _():
        bring(0)
        bring(1)
        qq, qd, dq, dd, qd_n2, dd_n2, dd_p2 = tiles[:7]
        qq_n2, dq_p2, qq_p2, qq_pair, cross_pair, dd_pair = tiles[7:13]
        qq_diag, cross_diag, dd_diag, qq_swap, dq_swap = tiles[13:]
        q_col = as_columns(lse[0:1, :])
        d_col = as_columns(lse[1:2, :])
        lane = lax.broadcasted_iota(jnp.int32, (size, size), 1)
        sublane = lax.broadcasted_iota(jnp.int32, (size, size), 0)
        pos_col = as_columns(pos[...])

        def put(target, slot, tile, column, row, taken=None):
            value = jnp.exp(tile - column) + jnp.exp(tile - row)
            if taken is not None:
                value = value - jnp.where(taken, 2.0, 0.0)
            target[:, slot * size : (slot + 1) * size] = value.astype(jnp.bfloat16)

        def q_of(ref):
            return ref[0:1, :]

        def d_of(ref):
            return ref[1:2, :]

        def pick(taken, yes, no):
            return jnp.where(taken, yes[...], no[...])

        put(coef_q, 0, pick(last, qq_swap, qq_n2), q_col, q_of(lse_n2))
        put(coef_q, 1, pick(even, qq_pair, qq_diag), q_col, q_of(lse_n1))
        put(coef_q, 2, qd[...], q_col, d_of(lse), pos_col == lane)
        put(coef_q, 3, qq[...], q_col, q_of(lse))
        put(coef_q, 4, qd_n2[...], q_col, d_of(lse_n2))
        put(coef_q, 5, pick(first, qq_swap, qq_p2), q_col, q_of(lse_p2))
        put(coef_q, 6, pick(even, cross_pair, cross_diag), q_col, d_of(lse_n1))
        put(coef_q, 7, pick(even, qq_diag, qq_pair), q_col, q_of(lse_p1))
        put(coef_d, 0, dd[...], d_col, d_of(lse))
        put(coef_d, 1, dq[...], d_col, q_of(lse), pos[...] == sublane)
        put(coef_d, 2, dd_n2[...], d_col, d_of(lse_n2))
        put(coef_d, 3, pick(first, dq_swap, dq_p2), d_col, q_of(lse_p2))
        put(coef_d, 4, pick(even, dd_pair, dd_diag), d_col, d_of(lse_n1))
        put(coef_d, 5, pick(even, cross_diag, cross_pair), d_col, q_of(lse_p1))
        put(coef_d, 6, dd_p2[...], d_col, d_of(lse_p2))
        put(coef_d, 7, pick(even, dd_diag, dd_pair), d_col, d_of(lse_p1))
        for part in range(2, parts):
            bring(part)

    pltpu.make_async_copy(rows.at[step], rows.at[step], arrived.at[step]).wait()
    depth = coef_q.shape[1]
    grad_q[...] = factor * jnp.dot(
        coef_q[...], rows[step, 0:depth, :], preferred_element_type=jnp.float32
    )
    grad_d[...] = factor * jnp.dot(
        coef_d[...], rows[step, 2 * size :, :], preferred_element_type=jnp.float32
    )


def per_device(queries, documents, positives):
    size, width = queries.shape
    count = lax.axis_size(AXES)
    scale = 2.0 / math.sqrt(width)
    factor = scale / (2.0 * size * count)
    own_block = lax.axis_index("dp") * lax.axis_size("inner") + lax.axis_index("inner")
    half, inner = count // 2, lax.axis_size("inner")
    within = own_block % half
    is_even = own_block % 2 == 0
    first, last = within < 2, within >= half - 2
    place = jnp.stack(
        [is_even, first, last, (within == 0) | (within == half - 1)]
    ).astype(jnp.int32)
    pos = (positives - own_block * size).reshape(1, size)
    index = jnp.arange(size)
    same_row = index[:, None] == index[None, :]
    down, up = down_hop(half), up_hop(half)
    barrier = lax.optimization_barrier

    def tile(left, right):
        return scale * contract(left, right)

    def masked(tile):
        return jnp.where(same_row, NEGATIVE, tile)

    q_down = sent(queries, down)
    d_up = sent(documents, up)
    d_p2 = sent(documents, lambda i: i + 2)
    d_n2 = sent(documents, lambda i: i - 2)
    q_edge = sent(
        queries,
        lambda i: i - 1 if i % half == 0 else i + 1,
        [0, half - 1, half, count - 1],
    )
    own_tiles = [
        masked(tile(queries, queries)),
        tile(queries, documents),
        tile(documents, queries),
        masked(tile(documents, documents)),
    ]
    q_down, d_up, own_tiles = barrier((q_down, d_up, own_tiles))
    q_pair = sent(q_down, down)
    d_pair = sent(d_up, up)
    q_own, d_p2, d_n2, q_edge, q_down, d_up = barrier((queries, d_p2, d_n2, q_edge, q_down, d_up))
    crossing = [i for i in range(count) if i % half < 2 or i % half >= half - 2]
    q_swap = sent(
        q_own, lambda i: i + half + (inner - 2 if i % half < 2 else 2 - inner), crossing
    )
    q_p2 = sent(q_own, lambda i: i + 2, [i for i in range(count) if i % half < half - 2])
    q_n2 = sent(q_own, lambda i: i - 2, [i for i in range(count) if i % half >= 2])
    far_tiles = [
        tile(queries, d_n2),
        tile(documents, d_n2),
        tile(documents, d_p2),
        tile(queries, q_edge),
        tile(documents, q_edge),
    ]
    cut = width // 2
    d_low = jnp.where(is_even, d_n2[:, :cut], d_p2[:, :cut])
    d_high = jnp.where(is_even, d_n2[:, cut:], d_p2[:, cut:])
    d_low, d_high, q_pair, d_pair, far_tiles = barrier((d_low, d_high, q_pair, d_pair, far_tiles))
    d_low = sent(d_low, up)
    d_high = sent(d_high, down)
    q_diag = sent(
        q_pair,
        lambda i: i - 2 if i % 2 else i + 2,
        [i for i in range(count) if i % half != 1 and i % half != half - 2],
    )
    d_low, d_high, q_swap, q_pair, d_pair, q_p2, q_n2 = barrier(
        (d_low, d_high, q_swap, q_pair, d_pair, q_p2, q_n2)
    )
    d_low = sent(d_low, up)
    d_high = sent(d_high, down)
    q_swap = sent(
        q_swap,
        lambda i: i + half - inner if i % half < inner else i - half + inner,
        [i for i in range(count) if i % half in (inner - 2, inner - 1, half - inner, half - inner + 1)],
    )

    in_vmem = pl.BlockSpec(memory_space=pltpu.VMEM)
    in_smem = pl.BlockSpec(memory_space=pltpu.SMEM)
    anywhere = pl.BlockSpec(memory_space=pl.ANY)
    column = jax.ShapeDtypeStruct((size, 128), jnp.float32)
    row = jax.ShapeDtypeStruct((1, size), jnp.float32)
    square = jax.ShapeDtypeStruct((size, size), jnp.float32)

    def early_tiles(*refs):
        early_kernel(scale, *refs)

    *early, q_max, q_sum, d_max, d_sum, positive = pl.pallas_call(
        early_tiles,
        out_shape=(square,) * 6 + (column,) * 4 + (row,),
        in_specs=[in_smem] + [in_vmem] * 14,
        out_specs=(in_vmem,) * 11,
        compiler_params=pltpu.CompilerParams(vmem_limit_bytes=SMALL_LIMIT),
        cost_estimate=pl.CostEstimate(
            flops=12 * size * size * width,
            bytes_accessed=12 * size * width,
            transcendentals=14 * size * size,
        ),
    )(
        place,
        pos,
        *own_tiles,
        *far_tiles[:3],
        queries,
        documents,
        q_n2,
        q_p2,
        q_pair,
        d_pair,
    )

    def last_tiles(*refs):
        lse_kernel(scale, *refs)

    *late, lse, row_terms = pl.pallas_call(
        last_tiles,
        out_shape=(square,) * 5 + (jax.ShapeDtypeStruct((2, size), jnp.float32), row),
        in_specs=[in_smem] + [in_vmem] * 13,
        out_specs=(in_vmem,) * 7,
        compiler_params=pltpu.CompilerParams(vmem_limit_bytes=SMALL_LIMIT),
        cost_estimate=pl.CostEstimate(
            flops=6 * size * size * width,
            bytes_accessed=8 * size * width,
            transcendentals=6 * size * size,
        ),
    )(
        place,
        far_tiles[3],
        far_tiles[4],
        q_max,
        q_sum,
        d_max,
        d_sum,
        positive,
        queries,
        documents,
        q_diag,
        d_low,
        d_high,
        q_swap,
    )
    tiles = [*own_tiles, *far_tiles[:3], *early, *late]
    lse_n1 = sent(lse, lambda i: i - 1)
    lse_p1 = sent(lse, lambda i: i + 1)
    lse_n2 = sent(lse, lambda i: i - 2)
    lse_p2 = sent(lse, lambda i: i + 2)
    sources = [queries, documents, q_n2, d_n2, q_p2, d_p2, q_pair, d_pair]
    sources += [q_edge, d_low, d_high, q_diag, q_swap]
    parts = width // CHUNK

    def kernel(*refs):
        grad_kernel(factor, *refs)

    grad_block = pl.BlockSpec((size, CHUNK), lambda step: (0, step))
    grad_q, grad_d = pl.pallas_call(
        kernel,
        grid=(parts,),
        out_shape=(jax.ShapeDtypeStruct((size, width), jnp.float32),) * 2,
        in_specs=[in_smem] + [in_vmem] * (6 + TILES) + [anywhere] * len(sources),
        out_specs=(grad_block, grad_block),
        scratch_shapes=[
            pltpu.VMEM((size, 8 * size), jnp.bfloat16),
            pltpu.VMEM((size, 8 * size), jnp.bfloat16),
            pltpu.VMEM((parts, 10 * size, CHUNK), jnp.bfloat16),
            pltpu.SemaphoreType.DMA((parts,)),
        ],
        compiler_params=pltpu.CompilerParams(vmem_limit_bytes=VMEM_LIMIT),
        cost_estimate=pl.CostEstimate(
            flops=2 * 16 * size * size * width,
            bytes_accessed=(20 + 8) * size * width,
            transcendentals=32 * size * size,
        ),
    )(place, pos, *tiles, lse, lse_n1, lse_p1, lse_n2, lse_p2, *sources)
    return (row_terms.reshape(size), grad_q, grad_d)


def solution(mesh):
    placed = (P(AXES, None), P(AXES, None), P(AXES))
    return jax.shard_map(
        per_device,
        mesh=mesh,
        in_specs=placed,
        out_specs=(P(AXES), P(AXES, None), P(AXES, None)),
        check_vma=False,
    )
```

```python
import math

import jax
import jax.numpy as jnp
from jax import lax
from jax.experimental import pallas as pl
from jax.experimental.pallas import tpu as pltpu
from jax.sharding import PartitionSpec as P

AXES = ("dp", "inner")
NEGATIVE = -1e30
CHUNK = 512
SLOTS = 4
VMEM_LIMIT = 20 * 1024 * 1024
SMALL_LIMIT = 14 * 1024 * 1024


def contract(left_rows, right_rows):
    return lax.dot_general(
        left_rows, right_rows, (((1,), (1,)), ((), ())), preferred_element_type=jnp.float32
    )


def sent(value, target, senders=None):
    count = lax.axis_size(AXES)
    senders = range(count) if senders is None else senders
    return lax.ppermute(value, AXES, [(i, target(i) % count) for i in senders])


def down_hop(half):
    return lambda i: i - half if i >= half else (i ^ 1) + half


def up_hop(half):
    return lambda i: (i - half) ^ 1 if i >= half else i + half


def as_columns(row):
    size = row.shape[1]
    return jnp.broadcast_to(row, (size, size)).T


def peak_and_sum(tiles):
    largest = tiles[0]
    for tile in tiles[1:]:
        largest = jnp.maximum(largest, tile)
    largest = jnp.max(largest, axis=1, keepdims=True)
    total = jnp.exp(tiles[0] - largest)
    for tile in tiles[1:]:
        total = total + jnp.exp(tile - largest)
    return largest, jnp.sum(total, axis=1, keepdims=True)


def early_kernel(scale, place, pos, *refs):
    qq, qd, dq, dd, qd_n2, dd_n2, dd_p2 = refs[:7]
    own_q, own_d, q_n2, q_p2, q_pair, d_pair = refs[7:13]
    qq_n2, dq_p2, qq_p2, qq_pair, cross_pair, dd_pair = refs[13:19]
    q_max, q_sum, d_max, d_sum, positive = refs[19:]
    even, first, last = [place[k] == 1 for k in range(3)]
    qq_pair[...] = scale * contract(own_q[...], q_pair[...])
    dd_pair[...] = scale * contract(own_d[...], d_pair[...])
    qq_n2[...] = scale * contract(own_q[...], q_n2[...])
    qq_p2[...] = scale * contract(own_q[...], q_p2[...])
    dq_p2[...] = scale * contract(own_d[...], q_p2[...])

    @pl.when(even)
    def _():
        cross_pair[...] = scale * contract(own_q[...], d_pair[...])

    @pl.when(jnp.logical_not(even))
    def _():
        cross_pair[...] = scale * contract(own_d[...], q_pair[...])

    cross = cross_pair[...]
    q_tiles = [
        qd[...],
        qq[...],
        qd_n2[...],
        qq_pair[...],
        jnp.where(last, NEGATIVE, qq_n2[...]),
        jnp.where(first, NEGATIVE, qq_p2[...]),
        jnp.where(even, cross, NEGATIVE),
    ]
    d_tiles = [
        dd[...],
        dq[...],
        dd_n2[...],
        dd_p2[...],
        dd_pair[...],
        jnp.where(first, NEGATIVE, dq_p2[...]),
        jnp.where(even, NEGATIVE, cross),
    ]
    for tiles, out_max, out_sum in ((q_tiles, q_max, q_sum), (d_tiles, d_max, d_sum)):
        largest, total = peak_and_sum(tiles)
        out_max[...] = jnp.broadcast_to(largest, out_max.shape)
        out_sum[...] = jnp.broadcast_to(total, out_sum.shape)
    doc = lax.broadcasted_iota(jnp.int32, dq.shape, 0)
    positive[...] = jnp.sum(jnp.where(doc == pos[...], dq[...], 0.0), axis=0, keepdims=True)


def lse_kernel(scale, place, qq_edge, dq_edge, q_max, q_sum, d_max, d_sum, positive, *refs):
    own_q, own_d, q_diag, d_low, d_high, q_swap = refs[:6]
    qq_diag, cross_diag, dd_diag, qq_swap, dq_swap, lse, row_terms = refs[6:]
    even, first, last, edge = [place[k] == 1 for k in range(4)]
    half = d_low.shape[1]

    def with_documents(own):
        return scale * (contract(own[:, :half], d_low[...]) + contract(own[:, half:], d_high[...]))

    qq_diag[...] = jnp.where(edge, qq_edge[...], scale * contract(own_q[...], q_diag[...]))
    dd_diag[...] = with_documents(own_d)

    @pl.when(even)
    def _():
        cross_diag[...] = jnp.where(edge, dq_edge[...], scale * contract(own_d[...], q_diag[...]))

    @pl.when(jnp.logical_not(even))
    def _():
        cross_diag[...] = with_documents(own_q)

    @pl.when(first | last)
    def _():
        qq_swap[...] = scale * contract(own_q[...], q_swap[...])
        dq_swap[...] = scale * contract(own_d[...], q_swap[...])

    @pl.when(jnp.logical_not(first | last))
    def _():
        qq_swap[...] = jnp.full(qq_swap.shape, NEGATIVE, jnp.float32)
        dq_swap[...] = jnp.full(dq_swap.shape, NEGATIVE, jnp.float32)

    def finished(early_max, early_sum, tiles):
        largest = early_max[:, :1]
        for tile in tiles:
            largest = jnp.maximum(largest, jnp.max(tile, axis=1, keepdims=True))
        total = jnp.exp(tiles[0] - largest)
        for tile in tiles[1:]:
            total = total + jnp.exp(tile - largest)
        total = jnp.sum(total, axis=1, keepdims=True)
        total = total + early_sum[:, :1] * jnp.exp(early_max[:, :1] - largest)
        return jnp.broadcast_to(largest + jnp.log(total), tiles[0].shape).T[:1]

    cross = cross_diag[...]
    q_late = [qq_diag[...], qq_swap[...], jnp.where(even, NEGATIVE, cross)]
    d_late = [dd_diag[...], jnp.where(first, dq_swap[...], NEGATIVE), jnp.where(even, cross, NEGATIVE)]
    q_row = finished(q_max, q_sum, q_late)
    d_row = finished(d_max, d_sum, d_late)
    lse[0:1, :] = q_row
    lse[1:2, :] = d_row
    row_terms[...] = q_row + d_row - 2.0 * positive[...]


TILES = 18


def grad_kernel(factor, place, pos, *refs):
    tiles, refs = refs[:TILES], refs[TILES:]
    lse, lse_n1, lse_p1, lse_n2, lse_p2 = refs[:5]
    own_q, own_d, q_n2, d_n2, q_p2, d_p2, q_pair, d_pair = refs[5:13]
    q_edge, d_low, d_high, q_diag, q_swap = refs[13:18]
    grad_q, grad_d, coef_q, coef_d, rows, arrived = refs[18:]
    step = pl.program_id(0)
    size = grad_q.shape[0]
    width = own_q.shape[1]
    chunk = rows.shape[2]
    parts = width // chunk
    even, first, last, edge = [place[k] == 1 for k in range(4)]

    def bring(part):
        held = part % SLOTS
        column = part * chunk if isinstance(part, int) else pl.multiple_of(part * chunk, chunk)

        def one(source, slot, column=column):
            start = slot * size if isinstance(slot, int) else pl.multiple_of(slot * size, size)
            pltpu.make_async_copy(
                source.at[:, pl.ds(column, chunk)],
                rows.at[held, pl.ds(start, size), :],
                arrived.at[held],
            ).start()

        def either(taken, yes, no, slot):
            pl.when(taken)(lambda: one(yes, slot))
            pl.when(jnp.logical_not(taken))(lambda: one(no, slot))

        one(own_d, 2)
        one(own_q, 3)
        one(d_n2, 4)
        one(d_p2, 8)
        one(q_pair, jnp.where(even, 1, 7))
        one(d_pair, jnp.where(even, 6, 9))
        d_slot = jnp.where(even, 9, 6)
        if isinstance(part, int):
            source = d_low if part < parts // 2 else d_high
            one(source, d_slot, part % (parts // 2) * chunk)
        else:
            inside = pl.multiple_of(part % (parts // 2) * chunk, chunk)
            pl.when(part < parts // 2)(lambda: one(d_low, d_slot, inside))
            pl.when(part >= parts // 2)(lambda: one(d_high, d_slot, inside))
        either(edge, q_edge, q_diag, jnp.where(even, 7, 1))
        either(last, q_swap, q_n2, 0)
        either(first, q_swap, q_p2, 5)

    @pl.when(step == 0)
    def _():
        for part in range(SLOTS - 1):
            bring(part)
        qq, qd, dq, dd, qd_n2, dd_n2, dd_p2 = tiles[:7]
        qq_n2, dq_p2, qq_p2, qq_pair, cross_pair, dd_pair = tiles[7:13]
        qq_diag, cross_diag, dd_diag, qq_swap, dq_swap = tiles[13:]
        q_col = as_columns(lse[0:1, :])
        d_col = as_columns(lse[1:2, :])
        lane = lax.broadcasted_iota(jnp.int32, (size, size), 1)
        sublane = lax.broadcasted_iota(jnp.int32, (size, size), 0)
        pos_col = as_columns(pos[...])

        def put(target, slot, tile, column, row, taken=None):
            value = jnp.exp(tile - column) + jnp.exp(tile - row)
            if taken is not None:
                value = value - jnp.where(taken, 2.0, 0.0)
            target[:, slot * size : (slot + 1) * size] = value.astype(jnp.bfloat16)

        def q_of(ref):
            return ref[0:1, :]

        def d_of(ref):
            return ref[1:2, :]

        def pick(taken, yes, no):
            return jnp.where(taken, yes[...], no[...])

        put(coef_q, 0, pick(last, qq_swap, qq_n2), q_col, q_of(lse_n2))
        put(coef_q, 1, pick(even, qq_pair, qq_diag), q_col, q_of(lse_n1))
        put(coef_q, 2, qd[...], q_col, d_of(lse), pos_col == lane)
        put(coef_q, 3, qq[...], q_col, q_of(lse))
        put(coef_q, 4, qd_n2[...], q_col, d_of(lse_n2))
        put(coef_q, 5, pick(first, qq_swap, qq_p2), q_col, q_of(lse_p2))
        put(coef_q, 6, pick(even, cross_pair, cross_diag), q_col, d_of(lse_n1))
        put(coef_q, 7, pick(even, qq_diag, qq_pair), q_col, q_of(lse_p1))
        put(coef_d, 0, dd[...], d_col, d_of(lse))
        put(coef_d, 1, dq[...], d_col, q_of(lse), pos[...] == sublane)
        put(coef_d, 2, dd_n2[...], d_col, d_of(lse_n2))
        put(coef_d, 3, pick(first, dq_swap, dq_p2), d_col, q_of(lse_p2))
        put(coef_d, 4, pick(even, dd_pair, dd_diag), d_col, d_of(lse_n1))
        put(coef_d, 5, pick(even, cross_diag, cross_pair), d_col, q_of(lse_p1))
        put(coef_d, 6, dd_p2[...], d_col, d_of(lse_p2))
        put(coef_d, 7, pick(even, dd_diag, dd_pair), d_col, d_of(lse_p1))

    @pl.when(step + SLOTS - 1 < parts)
    def _():
        bring(step + SLOTS - 1)

    held = step % SLOTS
    pltpu.make_async_copy(rows.at[held], rows.at[held], arrived.at[held]).wait()
    depth = coef_q.shape[1]
    grad_q[...] = factor * jnp.dot(
        coef_q[...], rows[held, 0:depth, :], preferred_element_type=jnp.float32
    )
    grad_d[...] = factor * jnp.dot(
        coef_d[...], rows[held, 2 * size :, :], preferred_element_type=jnp.float32
    )


def per_device(queries, documents, positives):
    size, width = queries.shape
    count = lax.axis_size(AXES)
    scale = 2.0 / math.sqrt(width)
    factor = scale / (2.0 * size * count)
    own_block = lax.axis_index("dp") * lax.axis_size("inner") + lax.axis_index("inner")
    half, inner = count // 2, lax.axis_size("inner")
    within = own_block % half
    is_even = own_block % 2 == 0
    first, last = within < 2, within >= half - 2
    place = jnp.stack(
        [is_even, first, last, (within == 0) | (within == half - 1)]
    ).astype(jnp.int32)
    pos = (positives - own_block * size).reshape(1, size)
    index = jnp.arange(size)
    same_row = index[:, None] == index[None, :]
    down, up = down_hop(half), up_hop(half)
    barrier = lax.optimization_barrier

    def tile(left, right):
        return scale * contract(left, right)

    def masked(tile):
        return jnp.where(same_row, NEGATIVE, tile)

    q_down = sent(queries, down)
    d_up = sent(documents, up)
    d_p2 = sent(documents, lambda i: i + 2)
    d_n2 = sent(documents, lambda i: i - 2)
    q_edge = sent(
        queries,
        lambda i: i - 1 if i % half == 0 else i + 1,
        [0, half - 1, half, count - 1],
    )
    own_tiles = [
        masked(tile(queries, queries)),
        tile(queries, documents),
        tile(documents, queries),
        masked(tile(documents, documents)),
    ]
    q_down, d_up, own_tiles = barrier((q_down, d_up, own_tiles))
    q_pair = sent(q_down, down)
    d_pair = sent(d_up, up)
    q_own, q_edge = barrier((queries, q_edge))
    q_p2 = sent(q_own, lambda i: i + 2, [i for i in range(count) if i % half < half - 2])
    q_own, d_n2 = barrier((queries, d_n2))
    q_n2 = sent(q_own, lambda i: i - 2, [i for i in range(count) if i % half >= 2])
    q_own, d_p2, d_n2, q_down, d_up = barrier((queries, d_p2, d_n2, q_down, d_up))
    crossing = [i for i in range(count) if i % half < 2 or i % half >= half - 2]
    q_swap = sent(
        q_own, lambda i: i + half + (inner - 2 if i % half < 2 else 2 - inner), crossing
    )
    far_tiles = [
        tile(queries, d_n2),
        tile(documents, d_n2),
        tile(documents, d_p2),
        tile(queries, q_edge),
        tile(documents, q_edge),
    ]
    cut = width // 2
    d_low = jnp.where(is_even, d_n2[:, :cut], d_p2[:, :cut])
    d_high = jnp.where(is_even, d_n2[:, cut:], d_p2[:, cut:])
    d_low, d_high, q_pair, d_pair, q_p2, q_n2, far_tiles = barrier(
        (d_low, d_high, q_pair, d_pair, q_p2, q_n2, far_tiles)
    )
    q_diag = sent(q_pair, lambda i: i - i % half + (i + (-2 if i % 2 else 2)) % half)
    d_low = sent(d_low, up)
    d_high = sent(d_high, down)
    d_low, d_high, q_swap, q_pair, d_pair, q_p2, q_n2 = barrier(
        (d_low, d_high, q_swap, q_pair, d_pair, q_p2, q_n2)
    )
    d_low = sent(d_low, up)
    d_high = sent(d_high, down)
    q_swap = sent(
        q_swap,
        lambda i: i + half - inner if i % half < inner else i - half + inner,
        [i for i in range(count) if i % half in (inner - 2, inner - 1, half - inner, half - inner + 1)],
    )

    in_vmem = pl.BlockSpec(memory_space=pltpu.VMEM)
    in_smem = pl.BlockSpec(memory_space=pltpu.SMEM)
    anywhere = pl.BlockSpec(memory_space=pl.ANY)
    column = jax.ShapeDtypeStruct((size, 128), jnp.float32)
    row = jax.ShapeDtypeStruct((1, size), jnp.float32)
    square = jax.ShapeDtypeStruct((size, size), jnp.float32)

    def early_tiles(*refs):
        early_kernel(scale, *refs)

    *early, q_max, q_sum, d_max, d_sum, positive = pl.pallas_call(
        early_tiles,
        out_shape=(square,) * 6 + (column,) * 4 + (row,),
        in_specs=[in_smem] + [in_vmem] * 14,
        out_specs=(in_vmem,) * 11,
        compiler_params=pltpu.CompilerParams(vmem_limit_bytes=SMALL_LIMIT),
        cost_estimate=pl.CostEstimate(
            flops=12 * size * size * width,
            bytes_accessed=12 * size * width,
            transcendentals=14 * size * size,
        ),
    )(
        place,
        pos,
        *own_tiles,
        *far_tiles[:3],
        queries,
        documents,
        q_n2,
        q_p2,
        q_pair,
        d_pair,
    )

    def last_tiles(*refs):
        lse_kernel(scale, *refs)

    *late, lse, row_terms = pl.pallas_call(
        last_tiles,
        out_shape=(square,) * 5 + (jax.ShapeDtypeStruct((2, size), jnp.float32), row),
        in_specs=[in_smem] + [in_vmem] * 13,
        out_specs=(in_vmem,) * 7,
        compiler_params=pltpu.CompilerParams(vmem_limit_bytes=SMALL_LIMIT),
        cost_estimate=pl.CostEstimate(
            flops=6 * size * size * width,
            bytes_accessed=8 * size * width,
            transcendentals=6 * size * size,
        ),
    )(
        place,
        far_tiles[3],
        far_tiles[4],
        q_max,
        q_sum,
        d_max,
        d_sum,
        positive,
        queries,
        documents,
        q_diag,
        d_low,
        d_high,
        q_swap,
    )
    tiles = [*own_tiles, *far_tiles[:3], *early, *late]
    lse_n1 = sent(lse, lambda i: i - 1)
    lse_p1 = sent(lse, lambda i: i + 1)
    lse_n2 = sent(lse, lambda i: i - 2)
    lse_p2 = sent(lse, lambda i: i + 2)
    sources = [queries, documents, q_n2, d_n2, q_p2, d_p2, q_pair, d_pair]
    sources += [q_edge, d_low, d_high, q_diag, q_swap]
    parts = width // CHUNK

    def kernel(*refs):
        grad_kernel(factor, *refs)

    grad_block = pl.BlockSpec((size, CHUNK), lambda step: (0, step))
    grad_q, grad_d = pl.pallas_call(
        kernel,
        grid=(parts,),
        out_shape=(jax.ShapeDtypeStruct((size, width), jnp.float32),) * 2,
        in_specs=[in_smem] + [in_vmem] * (6 + TILES) + [anywhere] * len(sources),
        out_specs=(grad_block, grad_block),
        scratch_shapes=[
            pltpu.VMEM((size, 8 * size), jnp.bfloat16),
            pltpu.VMEM((size, 8 * size), jnp.bfloat16),
            pltpu.VMEM((SLOTS, 10 * size, CHUNK), jnp.bfloat16),
            pltpu.SemaphoreType.DMA((SLOTS,)),
        ],
        compiler_params=pltpu.CompilerParams(vmem_limit_bytes=VMEM_LIMIT),
        cost_estimate=pl.CostEstimate(
            flops=2 * 16 * size * size * width,
            bytes_accessed=(20 + 8) * size * width,
            transcendentals=32 * size * size,
        ),
    )(place, pos, *tiles, lse, lse_n1, lse_p1, lse_n2, lse_p2, *sources)
    return (row_terms.reshape(size), grad_q, grad_d)


def solution(mesh):
    placed = (P(AXES, None), P(AXES, None), P(AXES))
    return jax.shard_map(
        per_device,
        mesh=mesh,
        in_specs=placed,
        out_specs=(P(AXES), P(AXES, None), P(AXES, None)),
        check_vma=False,
    )
```

```python
import math

import jax
import jax.numpy as jnp
from jax import lax
from jax.experimental import pallas as pl
from jax.experimental.pallas import tpu as pltpu
from jax.sharding import PartitionSpec as P

AXES = ("dp", "inner")
NEGATIVE = -1e30
CHUNK = 512
SLOTS = 4
VMEM_LIMIT = 50 * 1024 * 1024


def contract(left_rows, right_rows):
    return lax.dot_general(
        left_rows, right_rows, (((1,), (1,)), ((), ())), preferred_element_type=jnp.float32
    )


def sent(value, target, senders=None):
    count = lax.axis_size(AXES)
    senders = range(count) if senders is None else senders
    return lax.ppermute(value, AXES, [(i, target(i) % count) for i in senders])


def down_hop(half):
    return lambda i: i - half if i >= half else (i ^ 1) + half


def up_hop(half):
    return lambda i: (i - half) ^ 1 if i >= half else i + half


def as_columns(row):
    size = row.shape[1]
    return jnp.broadcast_to(row, (size, size)).T


def peak_and_sum(tiles):
    largest = tiles[0]
    for tile in tiles[1:]:
        largest = jnp.maximum(largest, tile)
    largest = jnp.max(largest, axis=1, keepdims=True)
    total = jnp.exp(tiles[0] - largest)
    for tile in tiles[1:]:
        total = total + jnp.exp(tile - largest)
    return largest, jnp.sum(total, axis=1, keepdims=True)


def early_kernel(scale, place, pos, *refs):
    qq, qd, dq, dd = refs[:4]
    sources = refs[4:12]
    qd_n2, dd_n2, dd_p2, qq_n2, dq_p2, qq_p2, qq_pair, cross_pair, dd_pair = refs[12:21]
    q_max, q_sum, d_max, d_sum, positive = refs[21:26]
    held, arrived = refs[26:]
    even, first, last = [place[k] == 1 for k in range(3)]
    copies = [
        pltpu.make_async_copy(source, held.at[k], arrived.at[k])
        for k, source in enumerate(sources)
    ]
    for copy in copies:
        copy.start()
    own_q, own_d, d_n2, d_p2, q_n2, q_p2, q_pair, d_pair = range(8)

    def product(left, right):
        return scale * contract(held[left], held[right])

    for k in (own_q, own_d, d_n2):
        copies[k].wait()
    qd_n2[...] = product(own_q, d_n2)
    dd_n2[...] = product(own_d, d_n2)
    copies[d_p2].wait()
    dd_p2[...] = product(own_d, d_p2)
    copies[q_n2].wait()
    qq_n2[...] = product(own_q, q_n2)
    copies[q_p2].wait()
    qq_p2[...] = product(own_q, q_p2)
    dq_p2[...] = product(own_d, q_p2)
    copies[q_pair].wait()
    qq_pair[...] = product(own_q, q_pair)
    copies[d_pair].wait()
    dd_pair[...] = product(own_d, d_pair)

    @pl.when(even)
    def _():
        cross_pair[...] = product(own_q, d_pair)

    @pl.when(jnp.logical_not(even))
    def _():
        cross_pair[...] = product(own_d, q_pair)

    cross = cross_pair[...]
    q_tiles = [
        qd[...],
        qq[...],
        qd_n2[...],
        qq_pair[...],
        jnp.where(last, NEGATIVE, qq_n2[...]),
        jnp.where(first, NEGATIVE, qq_p2[...]),
        jnp.where(even, cross, NEGATIVE),
    ]
    d_tiles = [
        dd[...],
        dq[...],
        dd_n2[...],
        dd_p2[...],
        dd_pair[...],
        jnp.where(first, NEGATIVE, dq_p2[...]),
        jnp.where(even, NEGATIVE, cross),
    ]
    for tiles, out_max, out_sum in ((q_tiles, q_max, q_sum), (d_tiles, d_max, d_sum)):
        largest, total = peak_and_sum(tiles)
        out_max[...] = jnp.broadcast_to(largest, out_max.shape)
        out_sum[...] = jnp.broadcast_to(total, out_sum.shape)
    doc = lax.broadcasted_iota(jnp.int32, dq.shape, 0)
    positive[...] = jnp.sum(jnp.where(doc == pos[...], dq[...], 0.0), axis=0, keepdims=True)


def lse_kernel(scale, place, q_max, q_sum, d_max, d_sum, positive, *refs):
    own_q, own_d, q_diag, q_edge, d_low, d_high, q_swap = refs[:7]
    qq_diag, cross_diag, dd_diag, qq_swap, dq_swap, lse, row_terms = refs[7:14]
    held, arrived = refs[14:]
    even, first, last, edge = [place[k] == 1 for k in range(4)]
    half = d_low.shape[1]
    crossed = first | last

    def copy(source, k, columns=slice(None)):
        return pltpu.make_async_copy(source, held.at[k, :, columns], arrived.at[k])

    low, high = slice(0, half), slice(half, 2 * half)
    copy(own_d, 0).start()
    copy(d_low, 1, low).start()
    copy(d_high, 1, high).start()
    copy(own_q, 2).start()
    pl.when(edge)(lambda: copy(q_edge, 3).start())
    pl.when(jnp.logical_not(edge))(lambda: copy(q_diag, 3).start())
    pl.when(crossed)(lambda: copy(q_swap, 4).start())

    def product(left, right):
        return scale * contract(held[left], held[right])

    copy(own_d, 0).wait()
    copy(own_d, 1).wait()
    dd_diag[...] = product(0, 1)
    copy(own_q, 2).wait()
    copy(q_diag, 3).wait()
    qq_diag[...] = product(2, 3)

    @pl.when(even)
    def _():
        cross_diag[...] = product(0, 3)

    @pl.when(jnp.logical_not(even))
    def _():
        cross_diag[...] = product(2, 1)

    @pl.when(crossed)
    def _():
        copy(q_swap, 4).wait()
        qq_swap[...] = product(2, 4)
        dq_swap[...] = product(0, 4)

    @pl.when(jnp.logical_not(crossed))
    def _():
        qq_swap[...] = jnp.full(qq_swap.shape, NEGATIVE, jnp.float32)
        dq_swap[...] = jnp.full(dq_swap.shape, NEGATIVE, jnp.float32)

    def finished(early_max, early_sum, tiles):
        largest = early_max[:, :1]
        for tile in tiles:
            largest = jnp.maximum(largest, jnp.max(tile, axis=1, keepdims=True))
        total = jnp.exp(tiles[0] - largest)
        for tile in tiles[1:]:
            total = total + jnp.exp(tile - largest)
        total = jnp.sum(total, axis=1, keepdims=True)
        total = total + early_sum[:, :1] * jnp.exp(early_max[:, :1] - largest)
        return jnp.broadcast_to(largest + jnp.log(total), tiles[0].shape).T[:1]

    cross = cross_diag[...]
    q_late = [qq_diag[...], qq_swap[...], jnp.where(even, NEGATIVE, cross)]
    d_late = [dd_diag[...], jnp.where(first, dq_swap[...], NEGATIVE), jnp.where(even, cross, NEGATIVE)]
    q_row = finished(q_max, q_sum, q_late)
    d_row = finished(d_max, d_sum, d_late)
    lse[0:1, :] = q_row
    lse[1:2, :] = d_row
    row_terms[...] = q_row + d_row - 2.0 * positive[...]


TILES = 18


def grad_kernel(factor, place, pos, *refs):
    tiles, refs = refs[:TILES], refs[TILES:]
    lse, lse_n1, lse_p1, lse_n2, lse_p2 = refs[:5]
    own_q, own_d, q_n2, d_n2, q_p2, d_p2, q_pair, d_pair = refs[5:13]
    q_edge, d_low, d_high, q_diag, q_swap = refs[13:18]
    grad_q, grad_d, coef_q, coef_d, rows, arrived = refs[18:]
    step = pl.program_id(0)
    size = grad_q.shape[0]
    width = own_q.shape[1]
    chunk = rows.shape[2]
    parts = width // chunk
    even, first, last, edge = [place[k] == 1 for k in range(4)]

    def bring(part):
        held = part % SLOTS
        column = part * chunk if isinstance(part, int) else pl.multiple_of(part * chunk, chunk)

        def one(source, slot, column=column):
            start = slot * size if isinstance(slot, int) else pl.multiple_of(slot * size, size)
            pltpu.make_async_copy(
                source.at[:, pl.ds(column, chunk)],
                rows.at[held, pl.ds(start, size), :],
                arrived.at[held],
            ).start()

        def either(taken, yes, no, slot):
            pl.when(taken)(lambda: one(yes, slot))
            pl.when(jnp.logical_not(taken))(lambda: one(no, slot))

        one(own_d, 2)
        one(own_q, 3)
        one(d_n2, 4)
        one(d_p2, 8)
        one(q_pair, jnp.where(even, 1, 7))
        one(d_pair, jnp.where(even, 6, 9))
        d_slot = jnp.where(even, 9, 6)
        if isinstance(part, int):
            source = d_low if part < parts // 2 else d_high
            one(source, d_slot, part % (parts // 2) * chunk)
        else:
            inside = pl.multiple_of(part % (parts // 2) * chunk, chunk)
            pl.when(part < parts // 2)(lambda: one(d_low, d_slot, inside))
            pl.when(part >= parts // 2)(lambda: one(d_high, d_slot, inside))
        either(edge, q_edge, q_diag, jnp.where(even, 7, 1))
        either(last, q_swap, q_n2, 0)
        either(first, q_swap, q_p2, 5)

    @pl.when(step == 0)
    def _():
        for part in range(SLOTS - 1):
            bring(part)
        qq, qd, dq, dd, qd_n2, dd_n2, dd_p2 = tiles[:7]
        qq_n2, dq_p2, qq_p2, qq_pair, cross_pair, dd_pair = tiles[7:13]
        qq_diag, cross_diag, dd_diag, qq_swap, dq_swap = tiles[13:]
        q_col = as_columns(lse[0:1, :])
        d_col = as_columns(lse[1:2, :])
        lane = lax.broadcasted_iota(jnp.int32, (size, size), 1)
        sublane = lax.broadcasted_iota(jnp.int32, (size, size), 0)
        pos_col = as_columns(pos[...])

        def put(target, slot, tile, column, row, taken=None):
            value = jnp.exp(tile - column) + jnp.exp(tile - row)
            if taken is not None:
                value = value - jnp.where(taken, 2.0, 0.0)
            target[:, slot * size : (slot + 1) * size] = value.astype(jnp.bfloat16)

        def q_of(ref):
            return ref[0:1, :]

        def d_of(ref):
            return ref[1:2, :]

        def pick(taken, yes, no):
            return jnp.where(taken, yes[...], no[...])

        put(coef_q, 0, pick(last, qq_swap, qq_n2), q_col, q_of(lse_n2))
        put(coef_q, 1, pick(even, qq_pair, qq_diag), q_col, q_of(lse_n1))
        put(coef_q, 2, qd[...], q_col, d_of(lse), pos_col == lane)
        put(coef_q, 3, qq[...], q_col, q_of(lse))
        put(coef_q, 4, qd_n2[...], q_col, d_of(lse_n2))
        put(coef_q, 5, pick(first, qq_swap, qq_p2), q_col, q_of(lse_p2))
        put(coef_q, 6, pick(even, cross_pair, cross_diag), q_col, d_of(lse_n1))
        put(coef_q, 7, pick(even, qq_diag, qq_pair), q_col, q_of(lse_p1))
        put(coef_d, 0, dd[...], d_col, d_of(lse))
        put(coef_d, 1, dq[...], d_col, q_of(lse), pos[...] == sublane)
        put(coef_d, 2, dd_n2[...], d_col, d_of(lse_n2))
        put(coef_d, 3, pick(first, dq_swap, dq_p2), d_col, q_of(lse_p2))
        put(coef_d, 4, pick(even, dd_pair, dd_diag), d_col, d_of(lse_n1))
        put(coef_d, 5, pick(even, cross_diag, cross_pair), d_col, q_of(lse_p1))
        put(coef_d, 6, dd_p2[...], d_col, d_of(lse_p2))
        put(coef_d, 7, pick(even, dd_diag, dd_pair), d_col, d_of(lse_p1))

    @pl.when(step + SLOTS - 1 < parts)
    def _():
        bring(step + SLOTS - 1)

    held = step % SLOTS
    pltpu.make_async_copy(rows.at[held], rows.at[held], arrived.at[held]).wait()
    depth = coef_q.shape[1]
    grad_q[...] = factor * jnp.dot(
        coef_q[...], rows[held, 0:depth, :], preferred_element_type=jnp.float32
    )
    grad_d[...] = factor * jnp.dot(
        coef_d[...], rows[held, 2 * size :, :], preferred_element_type=jnp.float32
    )


def per_device(queries, documents, positives):
    size, width = queries.shape
    count = lax.axis_size(AXES)
    scale = 2.0 / math.sqrt(width)
    factor = scale / (2.0 * size * count)
    own_block = lax.axis_index("dp") * lax.axis_size("inner") + lax.axis_index("inner")
    half, inner = count // 2, lax.axis_size("inner")
    within = own_block % half
    is_even = own_block % 2 == 0
    first, last = within < 2, within >= half - 2
    place = jnp.stack(
        [is_even, first, last, (within == 0) | (within == half - 1)]
    ).astype(jnp.int32)
    pos = (positives - own_block * size).reshape(1, size)
    index = jnp.arange(size)
    same_row = index[:, None] == index[None, :]
    down, up = down_hop(half), up_hop(half)
    barrier = lax.optimization_barrier

    def tile(left, right):
        return scale * contract(left, right)

    def masked(tile):
        return jnp.where(same_row, NEGATIVE, tile)

    q_down = sent(queries, down)
    d_up = sent(documents, up)
    q_p2 = sent(queries, lambda i: i + 2, [i for i in range(count) if i % half < half - 2])
    q_n2 = sent(queries, lambda i: i - 2, [i for i in range(count) if i % half >= 2])
    q_swap = sent(
        queries,
        lambda i: i + half + (inner - 2 if i % half < 2 else 2 - inner),
        [i for i in range(count) if i % half < 2 or i % half >= half - 2],
    )
    own_tiles = [
        masked(tile(queries, queries)),
        tile(queries, documents),
        tile(documents, queries),
        masked(tile(documents, documents)),
    ]
    q_down, d_up, own_tiles = barrier((q_down, d_up, own_tiles))
    q_pair = sent(q_down, down)
    d_pair = sent(d_up, up)
    d_own, q_p2, q_n2, q_down, d_up = barrier((documents, q_p2, q_n2, q_down, d_up))
    d_p2 = sent(d_own, lambda i: i + 2)
    d_n2 = sent(d_own, lambda i: i - 2)
    q_own, q_swap, q_p2, q_n2 = barrier((queries, q_swap, q_p2, q_n2))
    q_edge = sent(
        q_own,
        lambda i: i - 1 if i % half == 0 else i + 1,
        [0, half - 1, half, count - 1],
    )
    q_pair, d_pair = barrier((q_pair, d_pair))
    q_diag = sent(q_pair, lambda i: i - i % half + (i + (-2 if i % 2 else 2)) % half)
    d_p2, d_n2, q_pair, d_pair = barrier((d_p2, d_n2, q_pair, d_pair))
    cut = width // 2
    d_low = jnp.where(is_even, d_n2[:, :cut], d_p2[:, :cut])
    d_high = jnp.where(is_even, d_n2[:, cut:], d_p2[:, cut:])
    d_low, d_high, q_edge = barrier((d_low, d_high, q_edge))
    d_low = sent(d_low, up)
    d_high = sent(d_high, down)
    d_low, d_high, q_swap, q_pair, d_pair, q_p2, q_n2 = barrier(
        (d_low, d_high, q_swap, q_pair, d_pair, q_p2, q_n2)
    )
    d_low = sent(d_low, up)
    d_high = sent(d_high, down)
    q_swap = sent(
        q_swap,
        lambda i: i + half - inner if i % half < inner else i - half + inner,
        [i for i in range(count) if i % half in (inner - 2, inner - 1, half - inner, half - inner + 1)],
    )

    in_vmem = pl.BlockSpec(memory_space=pltpu.VMEM)
    in_smem = pl.BlockSpec(memory_space=pltpu.SMEM)
    anywhere = pl.BlockSpec(memory_space=pl.ANY)
    column = jax.ShapeDtypeStruct((size, 128), jnp.float32)
    row = jax.ShapeDtypeStruct((1, size), jnp.float32)
    square = jax.ShapeDtypeStruct((size, size), jnp.float32)

    def early_tiles(*refs):
        early_kernel(scale, *refs)

    *early, q_max, q_sum, d_max, d_sum, positive = pl.pallas_call(
        early_tiles,
        out_shape=(square,) * 9 + (column,) * 4 + (row,),
        in_specs=[in_smem] + [in_vmem] * 5 + [anywhere] * 8,
        out_specs=(in_vmem,) * 14,
        scratch_shapes=[
            pltpu.VMEM((8, size, width), jnp.bfloat16),
            pltpu.SemaphoreType.DMA((8,)),
        ],
        compiler_params=pltpu.CompilerParams(vmem_limit_bytes=VMEM_LIMIT),
        cost_estimate=pl.CostEstimate(
            flops=18 * size * size * width,
            bytes_accessed=16 * size * width,
            transcendentals=14 * size * size,
        ),
    )(place, pos, *own_tiles, queries, documents, d_n2, d_p2, q_n2, q_p2, q_pair, d_pair)

    def last_tiles(*refs):
        lse_kernel(scale, *refs)

    *late, lse, row_terms = pl.pallas_call(
        last_tiles,
        out_shape=(square,) * 5 + (jax.ShapeDtypeStruct((2, size), jnp.float32), row),
        in_specs=[in_smem] + [in_vmem] * 5 + [anywhere] * 7,
        out_specs=(in_vmem,) * 7,
        scratch_shapes=[
            pltpu.VMEM((5, size, width), jnp.bfloat16),
            pltpu.SemaphoreType.DMA((5,)),
        ],
        compiler_params=pltpu.CompilerParams(vmem_limit_bytes=VMEM_LIMIT),
        cost_estimate=pl.CostEstimate(
            flops=6 * size * size * width,
            bytes_accessed=8 * size * width,
            transcendentals=6 * size * size,
        ),
    )(
        place,
        q_max,
        q_sum,
        d_max,
        d_sum,
        positive,
        queries,
        documents,
        q_diag,
        q_edge,
        d_low,
        d_high,
        q_swap,
    )
    tiles = [*own_tiles, *early, *late]
    lse_n1 = sent(lse, lambda i: i - 1)
    lse_p1 = sent(lse, lambda i: i + 1)
    lse_n2 = sent(lse, lambda i: i - 2)
    lse_p2 = sent(lse, lambda i: i + 2)
    sources = [queries, documents, q_n2, d_n2, q_p2, d_p2, q_pair, d_pair]
    sources += [q_edge, d_low, d_high, q_diag, q_swap]
    parts = width // CHUNK

    def kernel(*refs):
        grad_kernel(factor, *refs)

    grad_block = pl.BlockSpec((size, CHUNK), lambda step: (0, step))
    grad_q, grad_d = pl.pallas_call(
        kernel,
        grid=(parts,),
        out_shape=(jax.ShapeDtypeStruct((size, width), jnp.float32),) * 2,
        in_specs=[in_smem] + [in_vmem] * (6 + TILES) + [anywhere] * len(sources),
        out_specs=(grad_block, grad_block),
        scratch_shapes=[
            pltpu.VMEM((size, 8 * size), jnp.bfloat16),
            pltpu.VMEM((size, 8 * size), jnp.bfloat16),
            pltpu.VMEM((SLOTS, 10 * size, CHUNK), jnp.bfloat16),
            pltpu.SemaphoreType.DMA((SLOTS,)),
        ],
        compiler_params=pltpu.CompilerParams(vmem_limit_bytes=VMEM_LIMIT),
        cost_estimate=pl.CostEstimate(
            flops=2 * 16 * size * size * width,
            bytes_accessed=(20 + 8) * size * width,
            transcendentals=32 * size * size,
        ),
    )(place, pos, *tiles, lse, lse_n1, lse_p1, lse_n2, lse_p2, *sources)
    return (row_terms.reshape(size), grad_q, grad_d)


def solution(mesh):
    placed = (P(AXES, None), P(AXES, None), P(AXES))
    return jax.shard_map(
        per_device,
        mesh=mesh,
        in_specs=placed,
        out_specs=(P(AXES), P(AXES, None), P(AXES, None)),
        check_vma=False,
    )
```

```python
import math

import jax
import jax.numpy as jnp
from jax import lax
from jax.experimental import pallas as pl
from jax.experimental.pallas import tpu as pltpu
from jax.sharding import PartitionSpec as P

AXES = ("dp", "inner")
NEGATIVE = -1e30
CHUNK = 512
SLOTS = 4
VMEM_LIMIT = 46 * 1024 * 1024
SMALL_LIMIT = 16 * 1024 * 1024


def contract(left_rows, right_rows):
    return lax.dot_general(
        left_rows, right_rows, (((1,), (1,)), ((), ())), preferred_element_type=jnp.float32
    )


def sent(value, target, senders=None):
    count = lax.axis_size(AXES)
    senders = range(count) if senders is None else senders
    return lax.ppermute(value, AXES, [(i, target(i) % count) for i in senders])


def down_hop(half):
    return lambda i: i - half if i >= half else (i ^ 1) + half


def up_hop(half):
    return lambda i: (i - half) ^ 1 if i >= half else i + half


def as_columns(row):
    size = row.shape[1]
    return jnp.broadcast_to(row, (size, size)).T


def peak_and_sum(tiles):
    largest = tiles[0]
    for tile in tiles[1:]:
        largest = jnp.maximum(largest, tile)
    largest = jnp.max(largest, axis=1, keepdims=True)
    total = jnp.exp(tiles[0] - largest)
    for tile in tiles[1:]:
        total = total + jnp.exp(tile - largest)
    return largest, jnp.sum(total, axis=1, keepdims=True)


def early_kernel(scale, place, pos, *refs):
    qq, qd, dq, dd, qd_n2, dd_n2, dd_p2 = refs[:7]
    own_q, own_d, q_n2, q_p2, q_pair, d_pair = refs[7:13]
    qq_n2, dq_p2, qq_p2, qq_pair, cross_pair, dd_pair = refs[13:19]
    q_max, q_sum, d_max, d_sum, positive = refs[19:]
    even, first, last = [place[k] == 1 for k in range(3)]
    qq_pair[...] = scale * contract(own_q[...], q_pair[...])
    dd_pair[...] = scale * contract(own_d[...], d_pair[...])
    qq_n2[...] = scale * contract(own_q[...], q_n2[...])
    qq_p2[...] = scale * contract(own_q[...], q_p2[...])
    dq_p2[...] = scale * contract(own_d[...], q_p2[...])

    @pl.when(even)
    def _():
        cross_pair[...] = scale * contract(own_q[...], d_pair[...])

    @pl.when(jnp.logical_not(even))
    def _():
        cross_pair[...] = scale * contract(own_d[...], q_pair[...])

    cross = cross_pair[...]
    q_tiles = [
        qd[...],
        qq[...],
        qd_n2[...],
        qq_pair[...],
        jnp.where(last, NEGATIVE, qq_n2[...]),
        jnp.where(first, NEGATIVE, qq_p2[...]),
        jnp.where(even, cross, NEGATIVE),
    ]
    d_tiles = [
        dd[...],
        dq[...],
        dd_n2[...],
        dd_p2[...],
        dd_pair[...],
        jnp.where(first, NEGATIVE, dq_p2[...]),
        jnp.where(even, NEGATIVE, cross),
    ]
    for tiles, out_max, out_sum in ((q_tiles, q_max, q_sum), (d_tiles, d_max, d_sum)):
        largest, total = peak_and_sum(tiles)
        out_max[...] = jnp.broadcast_to(largest, out_max.shape)
        out_sum[...] = jnp.broadcast_to(total, out_sum.shape)
    doc = lax.broadcasted_iota(jnp.int32, dq.shape, 0)
    positive[...] = jnp.sum(jnp.where(doc == pos[...], dq[...], 0.0), axis=0, keepdims=True)


def lse_kernel(scale, place, qq_edge, dq_edge, q_max, q_sum, d_max, d_sum, positive, *refs):
    own_q, own_d, q_diag, d_low, d_high, q_swap = refs[:6]
    qq_diag, cross_diag, dd_diag, qq_swap, dq_swap, lse, row_terms = refs[6:13]
    held, arrived = refs[13:]
    even, first, last, edge = [place[k] == 1 for k in range(4)]
    half = d_low.shape[1]
    crossed = first | last

    def copy(source, k, columns=slice(None)):
        return pltpu.make_async_copy(source, held.at[k, :, columns], arrived.at[k])

    copy(d_low, 0, slice(0, half)).start()
    copy(d_high, 0, slice(half, 2 * half)).start()
    copy(q_diag, 1).start()
    pl.when(crossed)(lambda: copy(q_swap, 2).start())

    def product(own, k):
        return scale * contract(own[...], held[k])

    pltpu.make_async_copy(held.at[0], held.at[0], arrived.at[0]).wait()
    dd_diag[...] = product(own_d, 0)
    copy(q_diag, 1).wait()
    qq_diag[...] = jnp.where(edge, qq_edge[...], product(own_q, 1))

    @pl.when(even)
    def _():
        cross_diag[...] = jnp.where(edge, dq_edge[...], product(own_d, 1))

    @pl.when(jnp.logical_not(even))
    def _():
        cross_diag[...] = product(own_q, 0)

    @pl.when(crossed)
    def _():
        copy(q_swap, 2).wait()
        qq_swap[...] = product(own_q, 2)
        dq_swap[...] = product(own_d, 2)

    @pl.when(jnp.logical_not(crossed))
    def _():
        qq_swap[...] = jnp.full(qq_swap.shape, NEGATIVE, jnp.float32)
        dq_swap[...] = jnp.full(dq_swap.shape, NEGATIVE, jnp.float32)

    def finished(early_max, early_sum, tiles):
        largest = early_max[:, :1]
        for tile in tiles:
            largest = jnp.maximum(largest, jnp.max(tile, axis=1, keepdims=True))
        total = jnp.exp(tiles[0] - largest)
        for tile in tiles[1:]:
            total = total + jnp.exp(tile - largest)
        total = jnp.sum(total, axis=1, keepdims=True)
        total = total + early_sum[:, :1] * jnp.exp(early_max[:, :1] - largest)
        return jnp.broadcast_to(largest + jnp.log(total), tiles[0].shape).T[:1]

    cross = cross_diag[...]
    q_late = [qq_diag[...], qq_swap[...], jnp.where(even, NEGATIVE, cross)]
    d_late = [dd_diag[...], jnp.where(first, dq_swap[...], NEGATIVE), jnp.where(even, cross, NEGATIVE)]
    q_row = finished(q_max, q_sum, q_late)
    d_row = finished(d_max, d_sum, d_late)
    lse[0:1, :] = q_row
    lse[1:2, :] = d_row
    row_terms[...] = q_row + d_row - 2.0 * positive[...]


TILES = 18


def grad_kernel(factor, place, pos, *refs):
    tiles, refs = refs[:TILES], refs[TILES:]
    lse, lse_n1, lse_p1, lse_n2, lse_p2 = refs[:5]
    own_q, own_d, q_n2, d_n2, q_p2, d_p2, q_pair, d_pair = refs[5:13]
    q_edge, d_low, d_high, q_diag, q_swap = refs[13:18]
    grad_q, grad_d, coef_both, coef_q, coef_d, rows, arrived = refs[18:]
    step = pl.program_id(0)
    size = grad_q.shape[0]
    width = own_q.shape[1]
    chunk = rows.shape[2]
    parts = width // chunk
    even, first, last, edge = [place[k] == 1 for k in range(4)]

    def bring(part):
        held = part % SLOTS
        column = part * chunk if isinstance(part, int) else pl.multiple_of(part * chunk, chunk)

        def one(source, slot, column=column):
            start = slot * size if isinstance(slot, int) else pl.multiple_of(slot * size, size)
            pltpu.make_async_copy(
                source.at[:, pl.ds(column, chunk)],
                rows.at[held, pl.ds(start, size), :],
                arrived.at[held],
            ).start()

        def either(taken, yes, no, slot):
            pl.when(taken)(lambda: one(yes, slot))
            pl.when(jnp.logical_not(taken))(lambda: one(no, slot))

        one(own_d, 2)
        one(own_q, 3)
        one(d_n2, 4)
        one(d_p2, 8)
        one(q_pair, jnp.where(even, 1, 7))
        one(d_pair, jnp.where(even, 6, 9))
        d_slot = jnp.where(even, 9, 6)
        if isinstance(part, int):
            source = d_low if part < parts // 2 else d_high
            one(source, d_slot, part % (parts // 2) * chunk)
        else:
            inside = pl.multiple_of(part % (parts // 2) * chunk, chunk)
            pl.when(part < parts // 2)(lambda: one(d_low, d_slot, inside))
            pl.when(part >= parts // 2)(lambda: one(d_high, d_slot, inside))
        either(edge, q_edge, q_diag, jnp.where(even, 7, 1))
        either(last, q_swap, q_n2, 0)
        either(first, q_swap, q_p2, 5)

    @pl.when(step == 0)
    def _():
        for part in range(SLOTS - 1):
            bring(part)
        qq, qd, dq, dd, qd_n2, dd_n2, dd_p2 = tiles[:7]
        qq_n2, dq_p2, qq_p2, qq_pair, cross_pair, dd_pair = tiles[7:13]
        qq_diag, cross_diag, dd_diag, qq_swap, dq_swap = tiles[13:]
        q_col = as_columns(lse[0:1, :])
        d_col = as_columns(lse[1:2, :])
        lane = lax.broadcasted_iota(jnp.int32, (size, size), 1)
        sublane = lax.broadcasted_iota(jnp.int32, (size, size), 0)
        pos_col = as_columns(pos[...])

        def put(target, slot, tile, column, row, taken=None):
            value = jnp.exp(tile - column) + jnp.exp(tile - row)
            if taken is not None:
                value = value - jnp.where(taken, 2.0, 0.0)
            taken_rows = slice(0, size)
            if target is coef_q and slot >= 2:
                target, slot = coef_both, slot - 2
            elif target is coef_d and slot < 6:
                target, taken_rows = coef_both, slice(size, 2 * size)
            elif target is coef_d:
                slot = slot - 6
            target[taken_rows, slot * size : (slot + 1) * size] = value.astype(jnp.bfloat16)

        def q_of(ref):
            return ref[0:1, :]

        def d_of(ref):
            return ref[1:2, :]

        def pick(taken, yes, no):
            return jnp.where(taken, yes[...], no[...])

        put(coef_q, 0, pick(last, qq_swap, qq_n2), q_col, q_of(lse_n2))
        put(coef_q, 1, pick(even, qq_pair, qq_diag), q_col, q_of(lse_n1))
        put(coef_q, 2, qd[...], q_col, d_of(lse), pos_col == lane)
        put(coef_q, 3, qq[...], q_col, q_of(lse))
        put(coef_q, 4, qd_n2[...], q_col, d_of(lse_n2))
        put(coef_q, 5, pick(first, qq_swap, qq_p2), q_col, q_of(lse_p2))
        put(coef_q, 6, pick(even, cross_pair, cross_diag), q_col, d_of(lse_n1))
        put(coef_q, 7, pick(even, qq_diag, qq_pair), q_col, q_of(lse_p1))
        put(coef_d, 0, dd[...], d_col, d_of(lse))
        put(coef_d, 1, dq[...], d_col, q_of(lse), pos[...] == sublane)
        put(coef_d, 2, dd_n2[...], d_col, d_of(lse_n2))
        put(coef_d, 3, pick(first, dq_swap, dq_p2), d_col, q_of(lse_p2))
        put(coef_d, 4, pick(even, dd_pair, dd_diag), d_col, d_of(lse_n1))
        put(coef_d, 5, pick(even, cross_diag, cross_pair), d_col, q_of(lse_p1))
        put(coef_d, 6, dd_p2[...], d_col, d_of(lse_p2))
        put(coef_d, 7, pick(even, dd_diag, dd_pair), d_col, d_of(lse_p1))

    @pl.when(step + SLOTS - 1 < parts)
    def _():
        bring(step + SLOTS - 1)

    held = step % SLOTS
    pltpu.make_async_copy(rows.at[held], rows.at[held], arrived.at[held]).wait()
    lone = 2 * size
    both = jnp.dot(
        coef_both[...], rows[held, lone : 4 * lone, :], preferred_element_type=jnp.float32
    )
    only_q = jnp.dot(coef_q[...], rows[held, 0:lone, :], preferred_element_type=jnp.float32)
    only_d = jnp.dot(coef_d[...], rows[held, 4 * lone :, :], preferred_element_type=jnp.float32)
    grad_q[...] = factor * (both[:size] + only_q)
    grad_d[...] = factor * (both[size:] + only_d)


def per_device(queries, documents, positives):
    size, width = queries.shape
    count = lax.axis_size(AXES)
    scale = 2.0 / math.sqrt(width)
    factor = scale / (2.0 * size * count)
    own_block = lax.axis_index("dp") * lax.axis_size("inner") + lax.axis_index("inner")
    half, inner = count // 2, lax.axis_size("inner")
    within = own_block % half
    is_even = own_block % 2 == 0
    first, last = within < 2, within >= half - 2
    place = jnp.stack(
        [is_even, first, last, (within == 0) | (within == half - 1)]
    ).astype(jnp.int32)
    pos = (positives - own_block * size).reshape(1, size)
    index = jnp.arange(size)
    same_row = index[:, None] == index[None, :]
    down, up = down_hop(half), up_hop(half)
    barrier = lax.optimization_barrier

    def tile(left, right):
        return scale * contract(left, right)

    def masked(tile):
        return jnp.where(same_row, NEGATIVE, tile)

    q_down = sent(queries, down)
    d_up = sent(documents, up)
    d_p2 = sent(documents, lambda i: i + 2)
    d_n2 = sent(documents, lambda i: i - 2)
    q_edge = sent(
        queries,
        lambda i: i - 1 if i % half == 0 else i + 1,
        [0, half - 1, half, count - 1],
    )
    own_tiles = [
        masked(tile(queries, queries)),
        tile(queries, documents),
        tile(documents, queries),
        masked(tile(documents, documents)),
    ]
    q_down, d_up, own_tiles = barrier((q_down, d_up, own_tiles))
    q_pair = sent(q_down, down)
    d_pair = sent(d_up, up)
    q_own, d_p2, d_n2, q_edge, q_down, d_up = barrier((queries, d_p2, d_n2, q_edge, q_down, d_up))
    crossing = [i for i in range(count) if i % half < 2 or i % half >= half - 2]
    q_swap = sent(
        q_own, lambda i: i + half + (inner - 2 if i % half < 2 else 2 - inner), crossing
    )
    q_p2 = sent(q_own, lambda i: i + 2, [i for i in range(count) if i % half < half - 2])
    q_n2 = sent(q_own, lambda i: i - 2, [i for i in range(count) if i % half >= 2])
    far_tiles = [
        tile(queries, d_n2),
        tile(documents, d_n2),
        tile(documents, d_p2),
        tile(queries, q_edge),
        tile(documents, q_edge),
    ]
    cut = width // 2
    d_low = jnp.where(is_even, d_n2[:, :cut], d_p2[:, :cut])
    d_high = jnp.where(is_even, d_n2[:, cut:], d_p2[:, cut:])
    d_low, d_high, q_pair, d_pair, far_tiles = barrier((d_low, d_high, q_pair, d_pair, far_tiles))
    d_low = sent(d_low, up)
    d_high = sent(d_high, down)
    q_diag = sent(
        q_pair,
        lambda i: i - 2 if i % 2 else i + 2,
        [i for i in range(count) if i % half != 1 and i % half != half - 2],
    )
    d_low, d_high, q_pair, d_pair, q_p2, q_n2 = barrier(
        (d_low, d_high, q_pair, d_pair, q_p2, q_n2)
    )
    d_low = sent(d_low, up)
    d_high = sent(d_high, down)
    q_swap = sent(
        q_swap,
        lambda i: i + half - inner if i % half < inner else i - half + inner,
        [i for i in range(count) if i % half in (inner - 2, inner - 1, half - inner, half - inner + 1)],
    )

    in_vmem = pl.BlockSpec(memory_space=pltpu.VMEM)
    in_smem = pl.BlockSpec(memory_space=pltpu.SMEM)
    anywhere = pl.BlockSpec(memory_space=pl.ANY)
    column = jax.ShapeDtypeStruct((size, 128), jnp.float32)
    row = jax.ShapeDtypeStruct((1, size), jnp.float32)
    square = jax.ShapeDtypeStruct((size, size), jnp.float32)

    def early_tiles(*refs):
        early_kernel(scale, *refs)

    *early, q_max, q_sum, d_max, d_sum, positive = pl.pallas_call(
        early_tiles,
        out_shape=(square,) * 6 + (column,) * 4 + (row,),
        in_specs=[in_smem] + [in_vmem] * 14,
        out_specs=(in_vmem,) * 11,
        compiler_params=pltpu.CompilerParams(vmem_limit_bytes=SMALL_LIMIT),
        cost_estimate=pl.CostEstimate(
            flops=12 * size * size * width,
            bytes_accessed=12 * size * width,
            transcendentals=14 * size * size,
        ),
    )(
        place,
        pos,
        *own_tiles,
        *far_tiles[:3],
        queries,
        documents,
        q_n2,
        q_p2,
        q_pair,
        d_pair,
    )

    def last_tiles(*refs):
        lse_kernel(scale, *refs)

    *late, lse, row_terms = pl.pallas_call(
        last_tiles,
        out_shape=(square,) * 5 + (jax.ShapeDtypeStruct((2, size), jnp.float32), row),
        in_specs=[in_smem] + [in_vmem] * 9 + [anywhere] * 4,
        out_specs=(in_vmem,) * 7,
        scratch_shapes=[
            pltpu.VMEM((3, size, width), jnp.bfloat16),
            pltpu.SemaphoreType.DMA((3,)),
        ],
        compiler_params=pltpu.CompilerParams(vmem_limit_bytes=VMEM_LIMIT),
        cost_estimate=pl.CostEstimate(
            flops=6 * size * size * width,
            bytes_accessed=8 * size * width,
            transcendentals=6 * size * size,
        ),
    )(
        place,
        far_tiles[3],
        far_tiles[4],
        q_max,
        q_sum,
        d_max,
        d_sum,
        positive,
        queries,
        documents,
        q_diag,
        d_low,
        d_high,
        q_swap,
    )
    tiles = [*own_tiles, *far_tiles[:3], *early, *late]
    lse_n1 = sent(lse, lambda i: i - 1)
    lse_p1 = sent(lse, lambda i: i + 1)
    lse_n2 = sent(lse, lambda i: i - 2)
    lse_p2 = sent(lse, lambda i: i + 2)
    sources = [queries, documents, q_n2, d_n2, q_p2, d_p2, q_pair, d_pair]
    sources += [q_edge, d_low, d_high, q_diag, q_swap]
    parts = width // CHUNK

    def kernel(*refs):
        grad_kernel(factor, *refs)

    grad_block = pl.BlockSpec((size, CHUNK), lambda step: (0, step))
    grad_q, grad_d = pl.pallas_call(
        kernel,
        grid=(parts,),
        out_shape=(jax.ShapeDtypeStruct((size, width), jnp.float32),) * 2,
        in_specs=[in_smem] + [in_vmem] * (6 + TILES) + [anywhere] * len(sources),
        out_specs=(grad_block, grad_block),
        scratch_shapes=[
            pltpu.VMEM((2 * size, 6 * size), jnp.bfloat16),
            pltpu.VMEM((size, 2 * size), jnp.bfloat16),
            pltpu.VMEM((size, 2 * size), jnp.bfloat16),
            pltpu.VMEM((SLOTS, 10 * size, CHUNK), jnp.bfloat16),
            pltpu.SemaphoreType.DMA((SLOTS,)),
        ],
        compiler_params=pltpu.CompilerParams(vmem_limit_bytes=VMEM_LIMIT),
        cost_estimate=pl.CostEstimate(
            flops=2 * 16 * size * size * width,
            bytes_accessed=(20 + 8) * size * width,
            transcendentals=32 * size * size,
        ),
    )(place, pos, *tiles, lse, lse_n1, lse_p1, lse_n2, lse_p2, *sources)
    return (row_terms.reshape(size), grad_q, grad_d)


def solution(mesh):
    placed = (P(AXES, None), P(AXES, None), P(AXES))
    return jax.shard_map(
        per_device,
        mesh=mesh,
        in_specs=placed,
        out_specs=(P(AXES), P(AXES, None), P(AXES, None)),
        check_vma=False,
    )
```

```python
import math

import jax
import jax.numpy as jnp
from jax import lax
from jax.experimental import pallas as pl
from jax.experimental.pallas import tpu as pltpu
from jax.sharding import PartitionSpec as P

AXES = ("dp", "inner")
NEGATIVE = -1e30
CHUNK = 512
SLOTS = 4
VMEM_LIMIT = 40 * 1024 * 1024
SMALL_LIMIT = 12 * 1024 * 1024


def contract(left_rows, right_rows):
    return lax.dot_general(
        left_rows, right_rows, (((1,), (1,)), ((), ())), preferred_element_type=jnp.float32
    )


def sent(value, target, senders=None):
    count = lax.axis_size(AXES)
    senders = range(count) if senders is None else senders
    return lax.ppermute(value, AXES, [(i, target(i) % count) for i in senders])


def down_hop(half):
    return lambda i: i - half if i >= half else (i ^ 1) + half


def up_hop(half):
    return lambda i: (i - half) ^ 1 if i >= half else i + half


def as_columns(row):
    size = row.shape[1]
    return jnp.broadcast_to(row, (size, size)).T


def peak_and_sum(tiles):
    largest = tiles[0]
    for tile in tiles[1:]:
        largest = jnp.maximum(largest, tile)
    largest = jnp.max(largest, axis=1, keepdims=True)
    total = jnp.exp(tiles[0] - largest)
    for tile in tiles[1:]:
        total = total + jnp.exp(tile - largest)
    return largest, jnp.sum(total, axis=1, keepdims=True)


def early_kernel(scale, place, pos, *refs):
    qq, qd, dq, dd, qd_n2, dd_n2, dd_p2 = refs[:7]
    sources = refs[7:13]
    qq_n2, dq_p2, qq_p2, qq_pair, cross_pair, dd_pair = refs[13:19]
    q_max, q_sum, d_max, d_sum, positive = refs[19:24]
    held, arrived = refs[24:]
    even, first, last = [place[k] == 1 for k in range(3)]
    copies = [
        pltpu.make_async_copy(source, held.at[k], arrived.at[k])
        for k, source in enumerate(sources)
    ]
    for copy in copies:
        copy.start()
    own_q, own_d, q_n2, q_p2, q_pair, d_pair = range(6)

    def product(left, right):
        return scale * contract(held[left], held[right])

    for k in (own_q, own_d, q_n2):
        copies[k].wait()
    qq_n2[...] = product(own_q, q_n2)
    copies[q_p2].wait()
    qq_p2[...] = product(own_q, q_p2)
    dq_p2[...] = product(own_d, q_p2)
    copies[q_pair].wait()
    qq_pair[...] = product(own_q, q_pair)
    copies[d_pair].wait()
    dd_pair[...] = product(own_d, d_pair)

    @pl.when(even)
    def _():
        cross_pair[...] = product(own_q, d_pair)

    @pl.when(jnp.logical_not(even))
    def _():
        cross_pair[...] = product(own_d, q_pair)

    cross = cross_pair[...]
    q_tiles = [
        qd[...],
        qq[...],
        qd_n2[...],
        qq_pair[...],
        jnp.where(last, NEGATIVE, qq_n2[...]),
        jnp.where(first, NEGATIVE, qq_p2[...]),
        jnp.where(even, cross, NEGATIVE),
    ]
    d_tiles = [
        dd[...],
        dq[...],
        dd_n2[...],
        dd_p2[...],
        dd_pair[...],
        jnp.where(first, NEGATIVE, dq_p2[...]),
        jnp.where(even, NEGATIVE, cross),
    ]
    for tiles, out_max, out_sum in ((q_tiles, q_max, q_sum), (d_tiles, d_max, d_sum)):
        largest, total = peak_and_sum(tiles)
        out_max[...] = jnp.broadcast_to(largest, out_max.shape)
        out_sum[...] = jnp.broadcast_to(total, out_sum.shape)
    doc = lax.broadcasted_iota(jnp.int32, dq.shape, 0)
    positive[...] = jnp.sum(jnp.where(doc == pos[...], dq[...], 0.0), axis=0, keepdims=True)


def lse_kernel(scale, place, qq_edge, dq_edge, q_max, q_sum, d_max, d_sum, positive, *refs):
    own_q, own_d, q_diag, d_low, d_high, q_swap = refs[:6]
    qq_diag, cross_diag, dd_diag, qq_swap, dq_swap, lse, row_terms, held, arrived = refs[6:]
    even, first, last, edge = [place[k] == 1 for k in range(4)]
    half = d_low.shape[1]
    copy = pltpu.make_async_copy(q_swap, held, arrived)
    pl.when(first | last)(copy.start)

    def with_documents(own):
        return scale * (contract(own[:, :half], d_low[...]) + contract(own[:, half:], d_high[...]))

    qq_diag[...] = jnp.where(edge, qq_edge[...], scale * contract(own_q[...], q_diag[...]))
    dd_diag[...] = with_documents(own_d)

    @pl.when(even)
    def _():
        cross_diag[...] = jnp.where(edge, dq_edge[...], scale * contract(own_d[...], q_diag[...]))

    @pl.when(jnp.logical_not(even))
    def _():
        cross_diag[...] = with_documents(own_q)

    @pl.when(first | last)
    def _():
        copy.wait()
        qq_swap[...] = scale * contract(own_q[...], held[...])
        dq_swap[...] = scale * contract(own_d[...], held[...])

    @pl.when(jnp.logical_not(first | last))
    def _():
        qq_swap[...] = jnp.full(qq_swap.shape, NEGATIVE, jnp.float32)
        dq_swap[...] = jnp.full(dq_swap.shape, NEGATIVE, jnp.float32)

    def finished(early_max, early_sum, tiles):
        largest = early_max[:, :1]
        for tile in tiles:
            largest = jnp.maximum(largest, jnp.max(tile, axis=1, keepdims=True))
        total = jnp.exp(tiles[0] - largest)
        for tile in tiles[1:]:
            total = total + jnp.exp(tile - largest)
        total = jnp.sum(total, axis=1, keepdims=True)
        total = total + early_sum[:, :1] * jnp.exp(early_max[:, :1] - largest)
        return jnp.broadcast_to(largest + jnp.log(total), tiles[0].shape).T[:1]

    cross = cross_diag[...]
    q_late = [qq_diag[...], qq_swap[...], jnp.where(even, NEGATIVE, cross)]
    d_late = [dd_diag[...], jnp.where(first, dq_swap[...], NEGATIVE), jnp.where(even, cross, NEGATIVE)]
    q_row = finished(q_max, q_sum, q_late)
    d_row = finished(d_max, d_sum, d_late)
    lse[0:1, :] = q_row
    lse[1:2, :] = d_row
    row_terms[...] = q_row + d_row - 2.0 * positive[...]


TILES = 18


def grad_kernel(factor, place, pos, *refs):
    tiles, refs = refs[:TILES], refs[TILES:]
    lse, lse_n1, lse_p1, lse_n2, lse_p2 = refs[:5]
    own_q, own_d, q_n2, d_n2, q_p2, d_p2, q_pair, d_pair = refs[5:13]
    q_edge, d_low, d_high, q_diag, q_swap = refs[13:18]
    grad_q, grad_d, coef_q, coef_d, rows, arrived = refs[18:]
    step = pl.program_id(0)
    size = grad_q.shape[0]
    width = own_q.shape[1]
    chunk = rows.shape[2]
    parts = width // chunk
    even, first, last, edge = [place[k] == 1 for k in range(4)]

    def bring(part):
        held = part % SLOTS
        column = part * chunk if isinstance(part, int) else pl.multiple_of(part * chunk, chunk)

        def one(source, slot, column=column):
            start = slot * size if isinstance(slot, int) else pl.multiple_of(slot * size, size)
            pltpu.make_async_copy(
                source.at[:, pl.ds(column, chunk)],
                rows.at[held, pl.ds(start, size), :],
                arrived.at[held],
            ).start()

        def either(taken, yes, no, slot):
            pl.when(taken)(lambda: one(yes, slot))
            pl.when(jnp.logical_not(taken))(lambda: one(no, slot))

        one(own_d, 2)
        one(own_q, 3)
        one(d_n2, 4)
        one(d_p2, 8)
        one(q_pair, jnp.where(even, 1, 7))
        one(d_pair, jnp.where(even, 6, 9))
        d_slot = jnp.where(even, 9, 6)
        if isinstance(part, int):
            source = d_low if part < parts // 2 else d_high
            one(source, d_slot, part % (parts // 2) * chunk)
        else:
            inside = pl.multiple_of(part % (parts // 2) * chunk, chunk)
            pl.when(part < parts // 2)(lambda: one(d_low, d_slot, inside))
            pl.when(part >= parts // 2)(lambda: one(d_high, d_slot, inside))
        either(edge, q_edge, q_diag, jnp.where(even, 7, 1))
        either(last, q_swap, q_n2, 0)
        either(first, q_swap, q_p2, 5)

    @pl.when(step == 0)
    def _():
        for part in range(SLOTS - 1):
            bring(part)
        qq, qd, dq, dd, qd_n2, dd_n2, dd_p2 = tiles[:7]
        qq_n2, dq_p2, qq_p2, qq_pair, cross_pair, dd_pair = tiles[7:13]
        qq_diag, cross_diag, dd_diag, qq_swap, dq_swap = tiles[13:]
        q_col = as_columns(lse[0:1, :])
        d_col = as_columns(lse[1:2, :])
        lane = lax.broadcasted_iota(jnp.int32, (size, size), 1)
        sublane = lax.broadcasted_iota(jnp.int32, (size, size), 0)
        pos_col = as_columns(pos[...])

        def put(target, slot, tile, column, row, taken=None):
            value = jnp.exp(tile - column) + jnp.exp(tile - row)
            if taken is not None:
                value = value - jnp.where(taken, 2.0, 0.0)
            target[:, slot * size : (slot + 1) * size] = value.astype(jnp.bfloat16)

        def q_of(ref):
            return ref[0:1, :]

        def d_of(ref):
            return ref[1:2, :]

        def pick(taken, yes, no):
            return jnp.where(taken, yes[...], no[...])

        put(coef_q, 0, pick(last, qq_swap, qq_n2), q_col, q_of(lse_n2))
        put(coef_q, 1, pick(even, qq_pair, qq_diag), q_col, q_of(lse_n1))
        put(coef_q, 2, qd[...], q_col, d_of(lse), pos_col == lane)
        put(coef_q, 3, qq[...], q_col, q_of(lse))
        put(coef_q, 4, qd_n2[...], q_col, d_of(lse_n2))
        put(coef_q, 5, pick(first, qq_swap, qq_p2), q_col, q_of(lse_p2))
        put(coef_q, 6, pick(even, cross_pair, cross_diag), q_col, d_of(lse_n1))
        put(coef_q, 7, pick(even, qq_diag, qq_pair), q_col, q_of(lse_p1))
        put(coef_d, 0, dd[...], d_col, d_of(lse))
        put(coef_d, 1, dq[...], d_col, q_of(lse), pos[...] == sublane)
        put(coef_d, 2, dd_n2[...], d_col, d_of(lse_n2))
        put(coef_d, 3, pick(first, dq_swap, dq_p2), d_col, q_of(lse_p2))
        put(coef_d, 4, pick(even, dd_pair, dd_diag), d_col, d_of(lse_n1))
        put(coef_d, 5, pick(even, cross_diag, cross_pair), d_col, q_of(lse_p1))
        put(coef_d, 6, dd_p2[...], d_col, d_of(lse_p2))
        put(coef_d, 7, pick(even, dd_diag, dd_pair), d_col, d_of(lse_p1))

    @pl.when(step + SLOTS - 1 < parts)
    def _():
        bring(step + SLOTS - 1)

    held = step % SLOTS
    pltpu.make_async_copy(rows.at[held], rows.at[held], arrived.at[held]).wait()
    depth = coef_q.shape[1]
    grad_q[...] = factor * jnp.dot(
        coef_q[...], rows[held, 0:depth, :], preferred_element_type=jnp.float32
    )
    grad_d[...] = factor * jnp.dot(
        coef_d[...], rows[held, 2 * size :, :], preferred_element_type=jnp.float32
    )


def per_device(queries, documents, positives):
    size, width = queries.shape
    count = lax.axis_size(AXES)
    scale = 2.0 / math.sqrt(width)
    factor = scale / (2.0 * size * count)
    own_block = lax.axis_index("dp") * lax.axis_size("inner") + lax.axis_index("inner")
    half, inner = count // 2, lax.axis_size("inner")
    within = own_block % half
    is_even = own_block % 2 == 0
    first, last = within < 2, within >= half - 2
    place = jnp.stack(
        [is_even, first, last, (within == 0) | (within == half - 1)]
    ).astype(jnp.int32)
    pos = (positives - own_block * size).reshape(1, size)
    index = jnp.arange(size)
    same_row = index[:, None] == index[None, :]
    down, up = down_hop(half), up_hop(half)
    barrier = lax.optimization_barrier

    def tile(left, right):
        return scale * contract(left, right)

    def masked(tile):
        return jnp.where(same_row, NEGATIVE, tile)

    q_down = sent(queries, down)
    d_up = sent(documents, up)
    d_p2 = sent(documents, lambda i: i + 2)
    d_n2 = sent(documents, lambda i: i - 2)
    q_edge = sent(
        queries,
        lambda i: i - 1 if i % half == 0 else i + 1,
        [0, half - 1, half, count - 1],
    )
    own_tiles = [
        masked(tile(queries, queries)),
        tile(queries, documents),
        tile(documents, queries),
        masked(tile(documents, documents)),
    ]
    q_down, d_up, own_tiles = barrier((q_down, d_up, own_tiles))
    q_pair = sent(q_down, down)
    d_pair = sent(d_up, up)
    q_own, d_p2, d_n2, q_edge, q_down, d_up = barrier((queries, d_p2, d_n2, q_edge, q_down, d_up))
    crossing = [i for i in range(count) if i % half < 2 or i % half >= half - 2]
    q_swap = sent(
        q_own, lambda i: i + half + (inner - 2 if i % half < 2 else 2 - inner), crossing
    )
    q_p2 = sent(q_own, lambda i: i + 2, [i for i in range(count) if i % half < half - 2])
    q_n2 = sent(q_own, lambda i: i - 2, [i for i in range(count) if i % half >= 2])
    far_tiles = [
        tile(queries, d_n2),
        tile(documents, d_n2),
        tile(documents, d_p2),
        tile(queries, q_edge),
        tile(documents, q_edge),
    ]
    cut = width // 2
    d_low = jnp.where(is_even, d_n2[:, :cut], d_p2[:, :cut])
    d_high = jnp.where(is_even, d_n2[:, cut:], d_p2[:, cut:])
    d_low, d_high, q_pair, d_pair, far_tiles = barrier((d_low, d_high, q_pair, d_pair, far_tiles))
    d_low = sent(d_low, up)
    d_high = sent(d_high, down)
    q_diag = sent(
        q_pair,
        lambda i: i - 2 if i % 2 else i + 2,
        [i for i in range(count) if i % half != 1 and i % half != half - 2],
    )
    d_low, d_high, q_swap, q_pair, d_pair, q_p2, q_n2 = barrier(
        (d_low, d_high, q_swap, q_pair, d_pair, q_p2, q_n2)
    )
    d_low = sent(d_low, up)
    d_high = sent(d_high, down)
    q_swap = sent(
        q_swap,
        lambda i: i + half - inner if i % half < inner else i - half + inner,
        [i for i in range(count) if i % half in (inner - 2, inner - 1, half - inner, half - inner + 1)],
    )

    in_vmem = pl.BlockSpec(memory_space=pltpu.VMEM)
    in_smem = pl.BlockSpec(memory_space=pltpu.SMEM)
    anywhere = pl.BlockSpec(memory_space=pl.ANY)
    column = jax.ShapeDtypeStruct((size, 128), jnp.float32)
    row = jax.ShapeDtypeStruct((1, size), jnp.float32)
    square = jax.ShapeDtypeStruct((size, size), jnp.float32)

    def early_tiles(*refs):
        early_kernel(scale, *refs)

    *early, q_max, q_sum, d_max, d_sum, positive = pl.pallas_call(
        early_tiles,
        out_shape=(square,) * 6 + (column,) * 4 + (row,),
        in_specs=[in_smem] + [in_vmem] * 8 + [anywhere] * 6,
        out_specs=(in_vmem,) * 11,
        scratch_shapes=[
            pltpu.VMEM((6, size, width), jnp.bfloat16),
            pltpu.SemaphoreType.DMA((6,)),
        ],
        compiler_params=pltpu.CompilerParams(vmem_limit_bytes=VMEM_LIMIT),
        cost_estimate=pl.CostEstimate(
            flops=12 * size * size * width,
            bytes_accessed=12 * size * width,
            transcendentals=14 * size * size,
        ),
    )(
        place,
        pos,
        *own_tiles,
        *far_tiles[:3],
        queries,
        documents,
        q_n2,
        q_p2,
        q_pair,
        d_pair,
    )

    def last_tiles(*refs):
        lse_kernel(scale, *refs)

    *late, lse, row_terms = pl.pallas_call(
        last_tiles,
        out_shape=(square,) * 5 + (jax.ShapeDtypeStruct((2, size), jnp.float32), row),
        in_specs=[in_smem] + [in_vmem] * 12 + [anywhere],
        out_specs=(in_vmem,) * 7,
        scratch_shapes=[pltpu.VMEM((size, width), jnp.bfloat16), pltpu.SemaphoreType.DMA],
        compiler_params=pltpu.CompilerParams(vmem_limit_bytes=SMALL_LIMIT),
        cost_estimate=pl.CostEstimate(
            flops=6 * size * size * width,
            bytes_accessed=8 * size * width,
            transcendentals=6 * size * size,
        ),
    )(
        place,
        far_tiles[3],
        far_tiles[4],
        q_max,
        q_sum,
        d_max,
        d_sum,
        positive,
        queries,
        documents,
        q_diag,
        d_low,
        d_high,
        q_swap,
    )
    tiles = [*own_tiles, *far_tiles[:3], *early, *late]
    lse_n1 = sent(lse, lambda i: i - 1)
    lse_p1 = sent(lse, lambda i: i + 1)
    lse_n2 = sent(lse, lambda i: i - 2)
    lse_p2 = sent(lse, lambda i: i + 2)
    sources = [queries, documents, q_n2, d_n2, q_p2, d_p2, q_pair, d_pair]
    sources += [q_edge, d_low, d_high, q_diag, q_swap]
    parts = width // CHUNK

    def kernel(*refs):
        grad_kernel(factor, *refs)

    grad_block = pl.BlockSpec((size, CHUNK), lambda step: (0, step))
    grad_q, grad_d = pl.pallas_call(
        kernel,
        grid=(parts,),
        out_shape=(jax.ShapeDtypeStruct((size, width), jnp.float32),) * 2,
        in_specs=[in_smem] + [in_vmem] * (6 + TILES) + [anywhere] * len(sources),
        out_specs=(grad_block, grad_block),
        scratch_shapes=[
            pltpu.VMEM((size, 8 * size), jnp.bfloat16),
            pltpu.VMEM((size, 8 * size), jnp.bfloat16),
            pltpu.VMEM((SLOTS, 10 * size, CHUNK), jnp.bfloat16),
            pltpu.SemaphoreType.DMA((SLOTS,)),
        ],
        compiler_params=pltpu.CompilerParams(vmem_limit_bytes=VMEM_LIMIT),
        cost_estimate=pl.CostEstimate(
            flops=2 * 16 * size * size * width,
            bytes_accessed=(20 + 8) * size * width,
            transcendentals=32 * size * size,
        ),
    )(place, pos, *tiles, lse, lse_n1, lse_p1, lse_n2, lse_p2, *sources)
    return (row_terms.reshape(size), grad_q, grad_d)


def solution(mesh):
    placed = (P(AXES, None), P(AXES, None), P(AXES))
    return jax.shard_map(
        per_device,
        mesh=mesh,
        in_specs=placed,
        out_specs=(P(AXES), P(AXES, None), P(AXES, None)),
        check_vma=False,
    )
```

```python
import math

import jax
import jax.numpy as jnp
from jax import lax
from jax.experimental import pallas as pl
from jax.experimental.pallas import tpu as pltpu
from jax.sharding import PartitionSpec as P

AXES = ("dp", "inner")
NEGATIVE = -1e30
CHUNK = 512
SLOTS = 4
VMEM_LIMIT = 20 * 1024 * 1024
SMALL_LIMIT = 12 * 1024 * 1024


def contract(left_rows, right_rows):
    return lax.dot_general(
        left_rows, right_rows, (((1,), (1,)), ((), ())), preferred_element_type=jnp.float32
    )


def sent(value, target, senders=None):
    count = lax.axis_size(AXES)
    senders = range(count) if senders is None else senders
    return lax.ppermute(value, AXES, [(i, target(i) % count) for i in senders])


def down_hop(half):
    return lambda i: i - half if i >= half else (i ^ 1) + half


def up_hop(half):
    return lambda i: (i - half) ^ 1 if i >= half else i + half


def as_columns(row):
    size = row.shape[1]
    return jnp.broadcast_to(row, (size, size)).T


def peak_and_sum(tiles):
    largest = tiles[0]
    for tile in tiles[1:]:
        largest = jnp.maximum(largest, tile)
    largest = jnp.max(largest, axis=1, keepdims=True)
    total = jnp.exp(tiles[0] - largest)
    for tile in tiles[1:]:
        total = total + jnp.exp(tile - largest)
    return largest, jnp.sum(total, axis=1, keepdims=True)


def early_kernel(scale, place, pos, *refs):
    qq, qd, dq, dd, qd_n2, dd_n2, dd_p2 = refs[:7]
    sources = refs[7:13]
    qq_n2, dq_p2, qq_p2, qq_pair, cross_pair, dd_pair = refs[13:19]
    q_max, q_sum, d_max, d_sum, positive = refs[19:24]
    held, arrived = refs[24:]
    even, first, last = [place[k] == 1 for k in range(3)]
    copies = [
        pltpu.make_async_copy(source, held.at[k], arrived.at[k])
        for k, source in enumerate(sources)
    ]
    for copy in copies:
        copy.start()
    own_q, own_d, q_n2, q_p2, q_pair, d_pair = range(6)

    def product(left, right):
        return scale * contract(held[left], held[right])

    for k in (own_q, own_d, q_n2):
        copies[k].wait()
    qq_n2[...] = product(own_q, q_n2)
    copies[q_p2].wait()
    qq_p2[...] = product(own_q, q_p2)
    dq_p2[...] = product(own_d, q_p2)
    copies[q_pair].wait()
    qq_pair[...] = product(own_q, q_pair)
    copies[d_pair].wait()
    dd_pair[...] = product(own_d, d_pair)

    @pl.when(even)
    def _():
        cross_pair[...] = product(own_q, d_pair)

    @pl.when(jnp.logical_not(even))
    def _():
        cross_pair[...] = product(own_d, q_pair)

    cross = cross_pair[...]
    q_tiles = [
        qd[...],
        qq[...],
        qd_n2[...],
        qq_pair[...],
        jnp.where(last, NEGATIVE, qq_n2[...]),
        jnp.where(first, NEGATIVE, qq_p2[...]),
        jnp.where(even, cross, NEGATIVE),
    ]
    d_tiles = [
        dd[...],
        dq[...],
        dd_n2[...],
        dd_p2[...],
        dd_pair[...],
        jnp.where(first, NEGATIVE, dq_p2[...]),
        jnp.where(even, NEGATIVE, cross),
    ]
    for tiles, out_max, out_sum in ((q_tiles, q_max, q_sum), (d_tiles, d_max, d_sum)):
        largest, total = peak_and_sum(tiles)
        out_max[...] = jnp.broadcast_to(largest, out_max.shape)
        out_sum[...] = jnp.broadcast_to(total, out_sum.shape)
    doc = lax.broadcasted_iota(jnp.int32, dq.shape, 0)
    positive[...] = jnp.sum(jnp.where(doc == pos[...], dq[...], 0.0), axis=0, keepdims=True)


def lse_kernel(scale, place, qq_edge, dq_edge, q_max, q_sum, d_max, d_sum, positive, *refs):
    own_q, own_d, q_diag, d_low, d_high, q_swap = refs[:6]
    qq_diag, cross_diag, dd_diag, qq_swap, dq_swap, lse, row_terms, held, arrived = refs[6:]
    even, first, last, edge = [place[k] == 1 for k in range(4)]
    half = d_low.shape[1]
    copy = pltpu.make_async_copy(q_swap, held, arrived)
    pl.when(first | last)(copy.start)

    def with_documents(own):
        return scale * (contract(own[:, :half], d_low[...]) + contract(own[:, half:], d_high[...]))

    qq_diag[...] = jnp.where(edge, qq_edge[...], scale * contract(own_q[...], q_diag[...]))
    dd_diag[...] = with_documents(own_d)

    @pl.when(even)
    def _():
        cross_diag[...] = jnp.where(edge, dq_edge[...], scale * contract(own_d[...], q_diag[...]))

    @pl.when(jnp.logical_not(even))
    def _():
        cross_diag[...] = with_documents(own_q)

    @pl.when(first | last)
    def _():
        copy.wait()
        qq_swap[...] = scale * contract(own_q[...], held[...])

    @pl.when(first)
    def _():
        dq_swap[...] = scale * contract(own_d[...], held[...])

    @pl.when(jnp.logical_not(first))
    def _():
        dq_swap[...] = jnp.full(dq_swap.shape, NEGATIVE, jnp.float32)

    @pl.when(jnp.logical_not(first | last))
    def _():
        qq_swap[...] = jnp.full(qq_swap.shape, NEGATIVE, jnp.float32)

    def finished(early_max, early_sum, tiles):
        largest = early_max[:, :1]
        for tile in tiles:
            largest = jnp.maximum(largest, jnp.max(tile, axis=1, keepdims=True))
        total = jnp.exp(tiles[0] - largest)
        for tile in tiles[1:]:
            total = total + jnp.exp(tile - largest)
        total = jnp.sum(total, axis=1, keepdims=True)
        total = total + early_sum[:, :1] * jnp.exp(early_max[:, :1] - largest)
        return jnp.broadcast_to(largest + jnp.log(total), tiles[0].shape).T[:1]

    cross = cross_diag[...]
    q_late = [qq_diag[...], qq_swap[...], jnp.where(even, NEGATIVE, cross)]
    d_late = [dd_diag[...], jnp.where(first, dq_swap[...], NEGATIVE), jnp.where(even, cross, NEGATIVE)]
    q_row = finished(q_max, q_sum, q_late)
    d_row = finished(d_max, d_sum, d_late)
    lse[0:1, :] = q_row
    lse[1:2, :] = d_row
    row_terms[...] = q_row + d_row - 2.0 * positive[...]


TILES = 18


def grad_kernel(factor, place, pos, *refs):
    tiles, refs = refs[:TILES], refs[TILES:]
    lse, lse_n1, lse_p1, lse_n2, lse_p2 = refs[:5]
    own_q, own_d, q_n2, d_n2, q_p2, d_p2, q_pair, d_pair = refs[5:13]
    q_edge, d_low, d_high, q_diag, q_swap = refs[13:18]
    grad_q, grad_d, coef_q, coef_d, rows, arrived = refs[18:]
    step = pl.program_id(0)
    size = grad_q.shape[0]
    width = own_q.shape[1]
    chunk = rows.shape[2]
    parts = width // chunk
    even, first, last, edge = [place[k] == 1 for k in range(4)]

    def bring(part):
        held = part % SLOTS
        column = part * chunk if isinstance(part, int) else pl.multiple_of(part * chunk, chunk)

        def one(source, slot, column=column):
            start = slot * size if isinstance(slot, int) else pl.multiple_of(slot * size, size)
            pltpu.make_async_copy(
                source.at[:, pl.ds(column, chunk)],
                rows.at[held, pl.ds(start, size), :],
                arrived.at[held],
            ).start()

        def either(taken, yes, no, slot):
            pl.when(taken)(lambda: one(yes, slot))
            pl.when(jnp.logical_not(taken))(lambda: one(no, slot))

        one(own_d, 2)
        one(own_q, 3)
        one(d_n2, 4)
        one(d_p2, 8)
        one(q_pair, jnp.where(even, 1, 7))
        one(d_pair, jnp.where(even, 6, 9))
        d_slot = jnp.where(even, 9, 6)
        if isinstance(part, int):
            source = d_low if part < parts // 2 else d_high
            one(source, d_slot, part % (parts // 2) * chunk)
        else:
            inside = pl.multiple_of(part % (parts // 2) * chunk, chunk)
            pl.when(part < parts // 2)(lambda: one(d_low, d_slot, inside))
            pl.when(part >= parts // 2)(lambda: one(d_high, d_slot, inside))
        either(edge, q_edge, q_diag, jnp.where(even, 7, 1))
        either(last, q_swap, q_n2, 0)
        either(first, q_swap, q_p2, 5)

    @pl.when(step == 0)
    def _():
        for part in range(SLOTS - 1):
            bring(part)
        qq, qd, dq, dd, qd_n2, dd_n2, dd_p2 = tiles[:7]
        qq_n2, dq_p2, qq_p2, qq_pair, cross_pair, dd_pair = tiles[7:13]
        qq_diag, cross_diag, dd_diag, qq_swap, dq_swap = tiles[13:]
        q_col = as_columns(lse[0:1, :])
        d_col = as_columns(lse[1:2, :])
        lane = lax.broadcasted_iota(jnp.int32, (size, size), 1)
        sublane = lax.broadcasted_iota(jnp.int32, (size, size), 0)
        pos_col = as_columns(pos[...])

        def put(target, slot, tile, column, row, taken=None):
            value = jnp.exp(tile - column) + jnp.exp(tile - row)
            if taken is not None:
                value = value - jnp.where(taken, 2.0, 0.0)
            target[:, slot * size : (slot + 1) * size] = value.astype(jnp.bfloat16)

        def q_of(ref):
            return ref[0:1, :]

        def d_of(ref):
            return ref[1:2, :]

        def pick(taken, yes, no):
            return jnp.where(taken, yes[...], no[...])

        put(coef_q, 0, pick(last, qq_swap, qq_n2), q_col, q_of(lse_n2))
        put(coef_q, 1, pick(even, qq_pair, qq_diag), q_col, q_of(lse_n1))
        put(coef_q, 2, qd[...], q_col, d_of(lse), pos_col == lane)
        put(coef_q, 3, qq[...], q_col, q_of(lse))
        put(coef_q, 4, qd_n2[...], q_col, d_of(lse_n2))
        put(coef_q, 5, pick(first, qq_swap, qq_p2), q_col, q_of(lse_p2))
        put(coef_q, 6, pick(even, cross_pair, cross_diag), q_col, d_of(lse_n1))
        put(coef_q, 7, pick(even, qq_diag, qq_pair), q_col, q_of(lse_p1))
        put(coef_d, 0, dd[...], d_col, d_of(lse))
        put(coef_d, 1, dq[...], d_col, q_of(lse), pos[...] == sublane)
        put(coef_d, 2, dd_n2[...], d_col, d_of(lse_n2))
        put(coef_d, 3, pick(first, dq_swap, dq_p2), d_col, q_of(lse_p2))
        put(coef_d, 4, pick(even, dd_pair, dd_diag), d_col, d_of(lse_n1))
        put(coef_d, 5, pick(even, cross_diag, cross_pair), d_col, q_of(lse_p1))
        put(coef_d, 6, dd_p2[...], d_col, d_of(lse_p2))
        put(coef_d, 7, pick(even, dd_diag, dd_pair), d_col, d_of(lse_p1))

    @pl.when(step + SLOTS - 1 < parts)
    def _():
        bring(step + SLOTS - 1)

    held = step % SLOTS
    pltpu.make_async_copy(rows.at[held], rows.at[held], arrived.at[held]).wait()
    depth = coef_q.shape[1]
    grad_q[...] = factor * jnp.dot(
        coef_q[...], rows[held, 0:depth, :], preferred_element_type=jnp.float32
    )
    grad_d[...] = factor * jnp.dot(
        coef_d[...], rows[held, 2 * size :, :], preferred_element_type=jnp.float32
    )


def per_device(queries, documents, positives):
    size, width = queries.shape
    count = lax.axis_size(AXES)
    scale = 2.0 / math.sqrt(width)
    factor = scale / (2.0 * size * count)
    own_block = lax.axis_index("dp") * lax.axis_size("inner") + lax.axis_index("inner")
    half, inner = count // 2, lax.axis_size("inner")
    within = own_block % half
    is_even = own_block % 2 == 0
    first, last = within < 2, within >= half - 2
    place = jnp.stack(
        [is_even, first, last, (within == 0) | (within == half - 1)]
    ).astype(jnp.int32)
    pos = (positives - own_block * size).reshape(1, size)
    index = jnp.arange(size)
    same_row = index[:, None] == index[None, :]
    down, up = down_hop(half), up_hop(half)
    barrier = lax.optimization_barrier

    def tile(left, right):
        return scale * contract(left, right)

    def masked(tile):
        return jnp.where(same_row, NEGATIVE, tile)

    q_down = sent(queries, down)
    d_up = sent(documents, up)
    d_p2 = sent(documents, lambda i: i + 2)
    d_n2 = sent(documents, lambda i: i - 2)
    q_edge = sent(
        queries,
        lambda i: i - 1 if i % half == 0 else i + 1,
        [0, half - 1, half, count - 1],
    )
    own_tiles = [
        masked(tile(queries, queries)),
        tile(queries, documents),
        tile(documents, queries),
        masked(tile(documents, documents)),
    ]
    q_down, d_up, own_tiles = barrier((q_down, d_up, own_tiles))
    q_pair = sent(q_down, down)
    d_pair = sent(d_up, up)
    q_own, d_p2, d_n2, q_edge, q_down, d_up = barrier((queries, d_p2, d_n2, q_edge, q_down, d_up))
    crossing = [i for i in range(count) if i % half < 2 or i % half >= half - 2]
    q_swap = sent(
        q_own, lambda i: i + half + (inner - 2 if i % half < 2 else 2 - inner), crossing
    )
    q_p2 = sent(q_own, lambda i: i + 2, [i for i in range(count) if i % half < half - 2])
    q_n2 = sent(q_own, lambda i: i - 2, [i for i in range(count) if i % half >= 2])
    far_tiles = [
        tile(queries, d_n2),
        tile(documents, d_n2),
        tile(documents, d_p2),
        tile(queries, q_edge),
        tile(documents, q_edge),
    ]
    cut = width // 2
    d_low = jnp.where(is_even, d_n2[:, :cut], d_p2[:, :cut])
    d_high = jnp.where(is_even, d_n2[:, cut:], d_p2[:, cut:])
    d_low, d_high, q_pair, d_pair, far_tiles = barrier((d_low, d_high, q_pair, d_pair, far_tiles))
    d_low = sent(d_low, up)
    d_high = sent(d_high, down)
    q_diag = sent(
        q_pair,
        lambda i: i - 2 if i % 2 else i + 2,
        [i for i in range(count) if i % half != 1 and i % half != half - 2],
    )
    d_low, d_high, q_swap, q_pair, d_pair, q_p2, q_n2 = barrier(
        (d_low, d_high, q_swap, q_pair, d_pair, q_p2, q_n2)
    )
    d_low = sent(d_low, up)
    d_high = sent(d_high, down)
    q_swap = sent(
        q_swap,
        lambda i: i + half - inner if i % half < inner else i - half + inner,
        [i for i in range(count) if i % half in (inner - 2, inner - 1, half - inner, half - inner + 1)],
    )

    in_vmem = pl.BlockSpec(memory_space=pltpu.VMEM)
    in_smem = pl.BlockSpec(memory_space=pltpu.SMEM)
    anywhere = pl.BlockSpec(memory_space=pl.ANY)
    column = jax.ShapeDtypeStruct((size, 128), jnp.float32)
    row = jax.ShapeDtypeStruct((1, size), jnp.float32)
    square = jax.ShapeDtypeStruct((size, size), jnp.float32)

    def early_tiles(*refs):
        early_kernel(scale, *refs)

    *early, q_max, q_sum, d_max, d_sum, positive = pl.pallas_call(
        early_tiles,
        out_shape=(square,) * 6 + (column,) * 4 + (row,),
        in_specs=[in_smem] + [in_vmem] * 8 + [anywhere] * 6,
        out_specs=(in_vmem,) * 11,
        scratch_shapes=[
            pltpu.VMEM((6, size, width), jnp.bfloat16),
            pltpu.SemaphoreType.DMA((6,)),
        ],
        compiler_params=pltpu.CompilerParams(vmem_limit_bytes=VMEM_LIMIT),
        cost_estimate=pl.CostEstimate(
            flops=12 * size * size * width,
            bytes_accessed=12 * size * width,
            transcendentals=14 * size * size,
        ),
    )(
        place,
        pos,
        *own_tiles,
        *far_tiles[:3],
        queries,
        documents,
        q_n2,
        q_p2,
        q_pair,
        d_pair,
    )

    def last_tiles(*refs):
        lse_kernel(scale, *refs)

    *late, lse, row_terms = pl.pallas_call(
        last_tiles,
        out_shape=(square,) * 5 + (jax.ShapeDtypeStruct((2, size), jnp.float32), row),
        in_specs=[in_smem] + [in_vmem] * 12 + [anywhere],
        out_specs=(in_vmem,) * 7,
        scratch_shapes=[pltpu.VMEM((size, width), jnp.bfloat16), pltpu.SemaphoreType.DMA],
        compiler_params=pltpu.CompilerParams(vmem_limit_bytes=SMALL_LIMIT),
        cost_estimate=pl.CostEstimate(
            flops=6 * size * size * width,
            bytes_accessed=8 * size * width,
            transcendentals=6 * size * size,
        ),
    )(
        place,
        far_tiles[3],
        far_tiles[4],
        q_max,
        q_sum,
        d_max,
        d_sum,
        positive,
        queries,
        documents,
        q_diag,
        d_low,
        d_high,
        q_swap,
    )
    tiles = [*own_tiles, *far_tiles[:3], *early, *late]
    lse_n1 = sent(lse, lambda i: i - 1)
    lse_p1 = sent(lse, lambda i: i + 1)
    lse_n2 = sent(lse, lambda i: i - 2)
    lse_p2 = sent(lse, lambda i: i + 2)
    sources = [queries, documents, q_n2, d_n2, q_p2, d_p2, q_pair, d_pair]
    sources += [q_edge, d_low, d_high, q_diag, q_swap]
    parts = width // CHUNK

    def kernel(*refs):
        grad_kernel(factor, *refs)

    grad_block = pl.BlockSpec((size, CHUNK), lambda step: (0, step))
    grad_q, grad_d = pl.pallas_call(
        kernel,
        grid=(parts,),
        out_shape=(jax.ShapeDtypeStruct((size, width), jnp.float32),) * 2,
        in_specs=[in_smem] + [in_vmem] * (6 + TILES) + [anywhere] * len(sources),
        out_specs=(grad_block, grad_block),
        scratch_shapes=[
            pltpu.VMEM((size, 8 * size), jnp.bfloat16),
            pltpu.VMEM((size, 8 * size), jnp.bfloat16),
            pltpu.VMEM((SLOTS, 10 * size, CHUNK), jnp.bfloat16),
            pltpu.SemaphoreType.DMA((SLOTS,)),
        ],
        compiler_params=pltpu.CompilerParams(vmem_limit_bytes=VMEM_LIMIT),
        cost_estimate=pl.CostEstimate(
            flops=2 * 16 * size * size * width,
            bytes_accessed=(20 + 8) * size * width,
            transcendentals=32 * size * size,
        ),
    )(place, pos, *tiles, lse, lse_n1, lse_p1, lse_n2, lse_p2, *sources)
    return (row_terms.reshape(size), grad_q, grad_d)


def solution(mesh):
    placed = (P(AXES, None), P(AXES, None), P(AXES))
    return jax.shard_map(
        per_device,
        mesh=mesh,
        in_specs=placed,
        out_specs=(P(AXES), P(AXES, None), P(AXES, None)),
        check_vma=False,
    )
```

```python
import math

import jax
import jax.numpy as jnp
from jax import lax
from jax.experimental import pallas as pl
from jax.experimental.pallas import tpu as pltpu
from jax.sharding import PartitionSpec as P

AXES = ("dp", "inner")
NEGATIVE = -1e30
CHUNK = 512
SLOTS = 4
VMEM_LIMIT = 40 * 1024 * 1024
SMALL_LIMIT = 12 * 1024 * 1024


def contract(left_rows, right_rows):
    return lax.dot_general(
        left_rows, right_rows, (((1,), (1,)), ((), ())), preferred_element_type=jnp.float32
    )


def sent(value, target, senders=None):
    count = lax.axis_size(AXES)
    senders = range(count) if senders is None else senders
    return lax.ppermute(value, AXES, [(i, target(i) % count) for i in senders])


def down_hop(half):
    return lambda i: i - half if i >= half else (i ^ 1) + half


def up_hop(half):
    return lambda i: (i - half) ^ 1 if i >= half else i + half


def as_columns(row):
    size = row.shape[1]
    return jnp.broadcast_to(row, (size, size)).T


def peak_and_sum(tiles):
    largest = tiles[0]
    for tile in tiles[1:]:
        largest = jnp.maximum(largest, tile)
    largest = jnp.max(largest, axis=1, keepdims=True)
    total = jnp.exp(tiles[0] - largest)
    for tile in tiles[1:]:
        total = total + jnp.exp(tile - largest)
    return largest, jnp.sum(total, axis=1, keepdims=True)


def early_kernel(scale, place, pos, *refs):
    qq, qd, dq, dd, qd_n2, dd_n2, dd_p2 = refs[:7]
    sources = refs[7:13]
    qq_n2, dq_p2, qq_p2, qq_pair, cross_pair, dd_pair = refs[13:19]
    q_max, q_sum, d_max, d_sum, positive = refs[19:24]
    held, arrived = refs[24:]
    even, first, last = [place[k] == 1 for k in range(3)]
    copies = [
        pltpu.make_async_copy(source, held.at[k], arrived.at[k])
        for k, source in enumerate(sources)
    ]
    for copy in copies:
        copy.start()
    own_q, own_d, q_n2, q_p2, q_pair, d_pair = range(6)

    def product(left, right):
        return scale * contract(held[left], held[right])

    for k in (own_q, own_d, q_n2):
        copies[k].wait()
    qq_n2[...] = product(own_q, q_n2)
    copies[q_p2].wait()
    qq_p2[...] = product(own_q, q_p2)
    dq_p2[...] = product(own_d, q_p2)
    copies[q_pair].wait()
    qq_pair[...] = product(own_q, q_pair)
    copies[d_pair].wait()
    dd_pair[...] = product(own_d, d_pair)

    @pl.when(even)
    def _():
        cross_pair[...] = product(own_q, d_pair)

    @pl.when(jnp.logical_not(even))
    def _():
        cross_pair[...] = product(own_d, q_pair)

    cross = cross_pair[...]
    q_tiles = [
        qd[...],
        qq[...],
        qd_n2[...],
        qq_pair[...],
        jnp.where(last, NEGATIVE, qq_n2[...]),
        jnp.where(first, NEGATIVE, qq_p2[...]),
        jnp.where(even, cross, NEGATIVE),
    ]
    d_tiles = [
        dd[...],
        dq[...],
        dd_n2[...],
        dd_p2[...],
        dd_pair[...],
        jnp.where(first, NEGATIVE, dq_p2[...]),
        jnp.where(even, NEGATIVE, cross),
    ]
    for tiles, out_max, out_sum in ((q_tiles, q_max, q_sum), (d_tiles, d_max, d_sum)):
        largest, total = peak_and_sum(tiles)
        out_max[...] = jnp.broadcast_to(largest, out_max.shape)
        out_sum[...] = jnp.broadcast_to(total, out_sum.shape)
    doc = lax.broadcasted_iota(jnp.int32, dq.shape, 0)
    positive[...] = jnp.sum(jnp.where(doc == pos[...], dq[...], 0.0), axis=0, keepdims=True)


def lse_kernel(scale, place, qq_edge, dq_edge, q_max, q_sum, d_max, d_sum, positive, *refs):
    own_q, own_d, q_diag, d_low, d_high, q_swap = refs[:6]
    qq_diag, cross_diag, dd_diag, qq_swap, dq_swap, lse, row_terms, held, arrived = refs[6:]
    even, first, last, edge = [place[k] == 1 for k in range(4)]
    half = d_low.shape[1]
    copy = pltpu.make_async_copy(q_swap, held, arrived)
    pl.when(first | last)(copy.start)

    def with_documents(own):
        return scale * (contract(own[:, :half], d_low[...]) + contract(own[:, half:], d_high[...]))

    qq_diag[...] = jnp.where(edge, qq_edge[...], scale * contract(own_q[...], q_diag[...]))
    dd_diag[...] = with_documents(own_d)

    @pl.when(even)
    def _():
        cross_diag[...] = jnp.where(edge, dq_edge[...], scale * contract(own_d[...], q_diag[...]))

    @pl.when(jnp.logical_not(even))
    def _():
        cross_diag[...] = with_documents(own_q)

    @pl.when(first | last)
    def _():
        copy.wait()
        qq_swap[...] = scale * contract(own_q[...], held[...])
        dq_swap[...] = scale * contract(own_d[...], held[...])

    @pl.when(jnp.logical_not(first | last))
    def _():
        qq_swap[...] = jnp.full(qq_swap.shape, NEGATIVE, jnp.float32)
        dq_swap[...] = jnp.full(dq_swap.shape, NEGATIVE, jnp.float32)

    def finished(early_max, early_sum, tiles):
        largest = early_max[:, :1]
        for tile in tiles:
            largest = jnp.maximum(largest, jnp.max(tile, axis=1, keepdims=True))
        total = jnp.exp(tiles[0] - largest)
        for tile in tiles[1:]:
            total = total + jnp.exp(tile - largest)
        total = jnp.sum(total, axis=1, keepdims=True)
        total = total + early_sum[:, :1] * jnp.exp(early_max[:, :1] - largest)
        return jnp.broadcast_to(largest + jnp.log(total), tiles[0].shape).T[:1]

    cross = cross_diag[...]
    q_late = [qq_diag[...], qq_swap[...], jnp.where(even, NEGATIVE, cross)]
    d_late = [dd_diag[...], jnp.where(first, dq_swap[...], NEGATIVE), jnp.where(even, cross, NEGATIVE)]
    q_row = finished(q_max, q_sum, q_late)
    d_row = finished(d_max, d_sum, d_late)
    lse[0:1, :] = q_row
    lse[1:2, :] = d_row
    row_terms[...] = q_row + d_row - 2.0 * positive[...]


TILES = 18


def grad_kernel(factor, place, pos, *refs):
    tiles, refs = refs[:TILES], refs[TILES:]
    lse, lse_n2, lse_p2, lse_n1, lse_p1 = refs[:5]
    own_q, own_d, q_n2, d_n2, q_p2, d_p2, q_pair, d_pair = refs[5:13]
    q_edge, d_low, d_high, q_diag, q_swap = refs[13:18]
    grad_q, grad_d, coef_q, coef_d, rows, arrived = refs[18:]
    step = pl.program_id(0)
    size = grad_q.shape[0]
    width = own_q.shape[1]
    chunk = rows.shape[2]
    parts = width // chunk
    even, first, last, edge = [place[k] == 1 for k in range(4)]

    def bring(part):
        held = part % SLOTS
        column = part * chunk if isinstance(part, int) else pl.multiple_of(part * chunk, chunk)

        def one(source, slot, column=column):
            start = slot * size if isinstance(slot, int) else pl.multiple_of(slot * size, size)
            pltpu.make_async_copy(
                source.at[:, pl.ds(column, chunk)],
                rows.at[held, pl.ds(start, size), :],
                arrived.at[held],
            ).start()

        def either(taken, yes, no, slot):
            pl.when(taken)(lambda: one(yes, slot))
            pl.when(jnp.logical_not(taken))(lambda: one(no, slot))

        one(own_d, 2)
        one(own_q, 3)
        one(d_n2, 4)
        one(d_p2, 8)
        one(q_pair, jnp.where(even, 1, 7))
        one(d_pair, jnp.where(even, 6, 9))
        d_slot = jnp.where(even, 9, 6)
        if isinstance(part, int):
            source = d_low if part < parts // 2 else d_high
            one(source, d_slot, part % (parts // 2) * chunk)
        else:
            inside = pl.multiple_of(part % (parts // 2) * chunk, chunk)
            pl.when(part < parts // 2)(lambda: one(d_low, d_slot, inside))
            pl.when(part >= parts // 2)(lambda: one(d_high, d_slot, inside))
        either(edge, q_edge, q_diag, jnp.where(even, 7, 1))
        either(last, q_swap, q_n2, 0)
        either(first, q_swap, q_p2, 5)

    @pl.when(step == 0)
    def _():
        for part in range(SLOTS - 1):
            bring(part)
        qq, qd, dq, dd, qd_n2, dd_n2, dd_p2 = tiles[:7]
        qq_n2, dq_p2, qq_p2, qq_pair, cross_pair, dd_pair = tiles[7:13]
        qq_diag, cross_diag, dd_diag, qq_swap, dq_swap = tiles[13:]
        q_col = as_columns(lse[0:1, :])
        d_col = as_columns(lse[1:2, :])
        lane = lax.broadcasted_iota(jnp.int32, (size, size), 1)
        sublane = lax.broadcasted_iota(jnp.int32, (size, size), 0)
        pos_col = as_columns(pos[...])

        def put(target, slot, tile, column, row, taken=None):
            value = jnp.exp(tile - column) + jnp.exp(tile - row)
            if taken is not None:
                value = value - jnp.where(taken, 2.0, 0.0)
            target[:, slot * size : (slot + 1) * size] = value.astype(jnp.bfloat16)

        def q_of(ref):
            return ref[0:1, :]

        def d_of(ref):
            return ref[1:2, :]

        def pick(taken, yes, no):
            return jnp.where(taken, yes[...], no[...])

        put(coef_q, 0, pick(last, qq_swap, qq_n2), q_col, q_of(lse_n2))
        put(coef_q, 1, pick(even, qq_pair, qq_diag), q_col, q_of(lse_n1))
        put(coef_q, 2, qd[...], q_col, d_of(lse), pos_col == lane)
        put(coef_q, 3, qq[...], q_col, q_of(lse))
        put(coef_q, 4, qd_n2[...], q_col, d_of(lse_n2))
        put(coef_q, 5, pick(first, qq_swap, qq_p2), q_col, q_of(lse_p2))
        put(coef_q, 6, pick(even, cross_pair, cross_diag), q_col, d_of(lse_n1))
        put(coef_q, 7, pick(even, qq_diag, qq_pair), q_col, q_of(lse_p1))
        put(coef_d, 0, dd[...], d_col, d_of(lse))
        put(coef_d, 1, dq[...], d_col, q_of(lse), pos[...] == sublane)
        put(coef_d, 2, dd_n2[...], d_col, d_of(lse_n2))
        put(coef_d, 3, pick(first, dq_swap, dq_p2), d_col, q_of(lse_p2))
        put(coef_d, 4, pick(even, dd_pair, dd_diag), d_col, d_of(lse_n1))
        put(coef_d, 5, pick(even, cross_diag, cross_pair), d_col, q_of(lse_p1))
        put(coef_d, 6, dd_p2[...], d_col, d_of(lse_p2))
        put(coef_d, 7, pick(even, dd_diag, dd_pair), d_col, d_of(lse_p1))

    @pl.when(step + SLOTS - 1 < parts)
    def _():
        bring(step + SLOTS - 1)

    held = step % SLOTS
    pltpu.make_async_copy(rows.at[held], rows.at[held], arrived.at[held]).wait()
    depth = coef_q.shape[1]
    grad_q[...] = factor * jnp.dot(
        coef_q[...], rows[held, 0:depth, :], preferred_element_type=jnp.float32
    )
    grad_d[...] = factor * jnp.dot(
        coef_d[...], rows[held, 2 * size :, :], preferred_element_type=jnp.float32
    )


def per_device(queries, documents, positives):
    size, width = queries.shape
    count = lax.axis_size(AXES)
    scale = 2.0 / math.sqrt(width)
    factor = scale / (2.0 * size * count)
    own_block = lax.axis_index("dp") * lax.axis_size("inner") + lax.axis_index("inner")
    half, inner = count // 2, lax.axis_size("inner")
    within = own_block % half
    is_even = own_block % 2 == 0
    first, last = within < 2, within >= half - 2
    place = jnp.stack(
        [is_even, first, last, (within == 0) | (within == half - 1)]
    ).astype(jnp.int32)
    pos = (positives - own_block * size).reshape(1, size)
    index = jnp.arange(size)
    same_row = index[:, None] == index[None, :]
    down, up = down_hop(half), up_hop(half)
    barrier = lax.optimization_barrier

    def tile(left, right):
        return scale * contract(left, right)

    def masked(tile):
        return jnp.where(same_row, NEGATIVE, tile)

    q_down = sent(queries, down)
    d_up = sent(documents, up)
    d_p2 = sent(documents, lambda i: i + 2)
    d_n2 = sent(documents, lambda i: i - 2)
    q_edge = sent(
        queries,
        lambda i: i - 1 if i % half == 0 else i + 1,
        [0, half - 1, half, count - 1],
    )
    own_tiles = [
        masked(tile(queries, queries)),
        tile(queries, documents),
        tile(documents, queries),
        masked(tile(documents, documents)),
    ]
    q_down, d_up, own_tiles = barrier((q_down, d_up, own_tiles))
    q_pair = sent(q_down, down)
    d_pair = sent(d_up, up)
    q_own, d_p2, d_n2, q_edge, q_down, d_up = barrier((queries, d_p2, d_n2, q_edge, q_down, d_up))
    crossing = [i for i in range(count) if i % half < 2 or i % half >= half - 2]
    q_swap = sent(
        q_own, lambda i: i + half + (inner - 2 if i % half < 2 else 2 - inner), crossing
    )
    q_p2 = sent(q_own, lambda i: i + 2, [i for i in range(count) if i % half < half - 2])
    q_n2 = sent(q_own, lambda i: i - 2, [i for i in range(count) if i % half >= 2])
    far_tiles = [
        tile(queries, d_n2),
        tile(documents, d_n2),
        tile(documents, d_p2),
        tile(queries, q_edge),
        tile(documents, q_edge),
    ]
    cut = width // 2
    d_low = jnp.where(is_even, d_n2[:, :cut], d_p2[:, :cut])
    d_high = jnp.where(is_even, d_n2[:, cut:], d_p2[:, cut:])
    d_low, d_high, q_pair, d_pair, far_tiles = barrier((d_low, d_high, q_pair, d_pair, far_tiles))
    d_low = sent(d_low, up)
    d_high = sent(d_high, down)
    q_diag = sent(
        q_pair,
        lambda i: i - 2 if i % 2 else i + 2,
        [i for i in range(count) if i % half != 1 and i % half != half - 2],
    )
    d_low, d_high, q_swap, q_pair, d_pair, q_p2, q_n2 = barrier(
        (d_low, d_high, q_swap, q_pair, d_pair, q_p2, q_n2)
    )
    d_low = sent(d_low, up)
    d_high = sent(d_high, down)
    q_swap = sent(
        q_swap,
        lambda i: i + half - inner if i % half < inner else i - half + inner,
        [i for i in range(count) if i % half in (inner - 2, inner - 1, half - inner, half - inner + 1)],
    )

    in_vmem = pl.BlockSpec(memory_space=pltpu.VMEM)
    in_smem = pl.BlockSpec(memory_space=pltpu.SMEM)
    anywhere = pl.BlockSpec(memory_space=pl.ANY)
    column = jax.ShapeDtypeStruct((size, 128), jnp.float32)
    row = jax.ShapeDtypeStruct((1, size), jnp.float32)
    square = jax.ShapeDtypeStruct((size, size), jnp.float32)

    def early_tiles(*refs):
        early_kernel(scale, *refs)

    *early, q_max, q_sum, d_max, d_sum, positive = pl.pallas_call(
        early_tiles,
        out_shape=(square,) * 6 + (column,) * 4 + (row,),
        in_specs=[in_smem] + [in_vmem] * 8 + [anywhere] * 6,
        out_specs=(in_vmem,) * 11,
        scratch_shapes=[
            pltpu.VMEM((6, size, width), jnp.bfloat16),
            pltpu.SemaphoreType.DMA((6,)),
        ],
        compiler_params=pltpu.CompilerParams(vmem_limit_bytes=VMEM_LIMIT),
        cost_estimate=pl.CostEstimate(
            flops=12 * size * size * width,
            bytes_accessed=12 * size * width,
            transcendentals=14 * size * size,
        ),
    )(
        place,
        pos,
        *own_tiles,
        *far_tiles[:3],
        queries,
        documents,
        q_n2,
        q_p2,
        q_pair,
        d_pair,
    )

    def last_tiles(*refs):
        lse_kernel(scale, *refs)

    *late, lse, row_terms = pl.pallas_call(
        last_tiles,
        out_shape=(square,) * 5 + (jax.ShapeDtypeStruct((2, size), jnp.float32), row),
        in_specs=[in_smem] + [in_vmem] * 12 + [anywhere],
        out_specs=(in_vmem,) * 7,
        scratch_shapes=[pltpu.VMEM((size, width), jnp.bfloat16), pltpu.SemaphoreType.DMA],
        compiler_params=pltpu.CompilerParams(vmem_limit_bytes=SMALL_LIMIT),
        cost_estimate=pl.CostEstimate(
            flops=6 * size * size * width,
            bytes_accessed=8 * size * width,
            transcendentals=6 * size * size,
        ),
    )(
        place,
        far_tiles[3],
        far_tiles[4],
        q_max,
        q_sum,
        d_max,
        d_sum,
        positive,
        queries,
        documents,
        q_diag,
        d_low,
        d_high,
        q_swap,
    )
    tiles = [*own_tiles, *far_tiles[:3], *early, *late]
    lse_n2 = sent(lse, lambda i: i - 2)
    lse_p2 = sent(lse, lambda i: i + 2)
    lse_n1 = sent(lse, lambda i: i - 1)
    lse_p1 = sent(lse, lambda i: i + 1)
    sources = [queries, documents, q_n2, d_n2, q_p2, d_p2, q_pair, d_pair]
    sources += [q_edge, d_low, d_high, q_diag, q_swap]
    parts = width // CHUNK

    def kernel(*refs):
        grad_kernel(factor, *refs)

    grad_block = pl.BlockSpec((size, CHUNK), lambda step: (0, step))
    grad_q, grad_d = pl.pallas_call(
        kernel,
        grid=(parts,),
        out_shape=(jax.ShapeDtypeStruct((size, width), jnp.float32),) * 2,
        in_specs=[in_smem] + [in_vmem] * (6 + TILES) + [anywhere] * len(sources),
        out_specs=(grad_block, grad_block),
        scratch_shapes=[
            pltpu.VMEM((size, 8 * size), jnp.bfloat16),
            pltpu.VMEM((size, 8 * size), jnp.bfloat16),
            pltpu.VMEM((SLOTS, 10 * size, CHUNK), jnp.bfloat16),
            pltpu.SemaphoreType.DMA((SLOTS,)),
        ],
        compiler_params=pltpu.CompilerParams(vmem_limit_bytes=VMEM_LIMIT),
        cost_estimate=pl.CostEstimate(
            flops=2 * 16 * size * size * width,
            bytes_accessed=(20 + 8) * size * width,
            transcendentals=32 * size * size,
        ),
    )(place, pos, *tiles, lse, lse_n2, lse_p2, lse_n1, lse_p1, *sources)
    return (row_terms.reshape(size), grad_q, grad_d)


def solution(mesh):
    placed = (P(AXES, None), P(AXES, None), P(AXES))
    return jax.shard_map(
        per_device,
        mesh=mesh,
        in_specs=placed,
        out_specs=(P(AXES), P(AXES, None), P(AXES, None)),
        check_vma=False,
    )
```
